512 devices in a mesh: pp: 8 (over x, y_lo), ep: 64 (over z, y_hi, core).
Axes of the slice: x: 4, y: 8 (y_hi: 4, y_lo: 2; y = y_hi * 2 + y_lo), z: 8, core: 2. Of those that a mesh axis runs over, the one named last changes fastest.
Arguments:
- forward_acts: bfloat16 [8, 1536, 3584], P('pp', 'ep'), may hold values from -6 to 6
- backward_grads: bfloat16 [8, 1536, 3584], P('pp', 'ep'), may hold values from -6 to 6
- forward_routes: int32 [8, 1536, 2], P('pp', 'ep'), may hold values from 0 to 7, all different within a row; in each aligned block of 24 rows (0 to 23, 24 to 47, ..., all dimensions but the last counted through in order) at most 8 rows name the same one
- backward_routes: int32 [8, 1536, 2], P('pp', 'ep'), may hold values from 0 to 7, all different within a row; in each aligned block of 24 rows (0 to 23, 24 to 47, ..., all dimensions but the last counted through in order) at most 8 rows name the same one
- forward_gates: float32 [8, 1536, 2], P('pp', 'ep'), may hold values from 0.3 to 1.5
- backward_gates: float32 [8, 1536, 2], P('pp', 'ep'), may hold values from 0.3 to 1.5
- gate_weight: bfloat16 [8, 3584, 8192], P('pp', None, 'ep'), may hold values from -0.09375 to 0.09375
- up_weight: bfloat16 [8, 3584, 8192], P('pp', None, 'ep'), may hold values from -0.09375 to 0.09375
- down_weight: bfloat16 [8, 8192, 3584], P('pp', 'ep'), may hold values from -0.1875 to 0.1875
- stashed_pre: bfloat16 [8, 64, 64, 8, 2, 128], P('pp', 'ep'), may hold values from -5 to 5
Outputs:
- forward_next: bfloat16 [8, 1536, 3584], P('pp', 'ep')
- backward_next: bfloat16 [8, 1536, 3584], P('pp', 'ep')
The draws below stay inside these ranges and needn't reach their ends.
Inputs may be any that keep to these rules, and one draw needn't show every extreme that they name: `forward_routes`: each token names 2 different experts; among the 24 tokens of one device at one section no expert is named more than 8 times, and some expert exactly that often. `backward_routes`: as for forward_routes.
All inputs are finite; a program needn't handle non-finite values.
Results may differ from the reference program's by a relative error of at most 0.0055.
Values may be sent and summed in bfloat16 or wider, within the bound.
A program may use at most 64 MiB of HBM per device.

```python
import math
import jax
import jax.numpy as jnp
import numpy as np
from jax import lax

D = 3584
HID = 1024
GROUP = 8
TOPK = 2
TOK_DEV = 24
EXPERTS = 8
HID_DEV = 128
CAP = 8
ROUTE_MOST = 8
TOKENS = 1536
N_PP = 8
N_EP = 64


def levels(rng, shape, split, least, high):
    loudness, own = 1.0, jax.random.fold_in(rng, 6)
    for position, shards_of in split:
        heights = jnp.exp(jax.random.uniform(jax.random.fold_in(own, position), (shards_of,), jnp.float32, least / len(split), high / len(split)))
        loudness = loudness * jnp.repeat(heights, shape[position] // shards_of).reshape([-1 if axis == position else 1 for axis in range(len(shape))])
    return loudness


def assign_block(rng, own, number, rows, amount, top, bound, slope):
    sequence = jax.random.permutation(rng, amount)
    packed, usual = load_shares(amount, rows * top, bound, slope, True), load_shares(amount, rows * top, bound, slope, False)
    places = jnp.arange(amount)

    def named(lengths, rotation):
        used = int((lengths > 0).sum())
        fixed = max(1, used // 4)
        shifted = fixed + (places - fixed + rotation * (used - fixed)) % max(1, amount - fixed)
        return jnp.zeros((amount,), jnp.int32).at[sequence[jnp.where(places < fixed, places, shifted)]].set(jnp.asarray(lengths, jnp.int32))

    lengths = jnp.where(number % 4 == 0, named(packed, number // 4), named(usual, number - number // 4 - 1))
    mixed = jax.random.permutation(jax.random.fold_in(own, 3), amount)
    donor, sink = mixed[0:amount // 2 * 2:2], mixed[1:amount // 2 * 2:2]
    room = jnp.minimum(lengths[donor] - 1, bound - lengths[sink]) // 2
    room = jnp.where((donor == sequence[0]) | (sink == sequence[0]) | (lengths[sink] == 0), 0, jnp.maximum(room, 0))
    shifted = jax.random.randint(jax.random.fold_in(own, 4), (amount // 2,), 0, 1 << 20) % (room + 1)
    lengths = lengths.at[donor].add(-shifted).at[sink].add(shifted)
    labels = jnp.searchsorted(jnp.cumsum(lengths), jnp.arange(rows * top), side="right").astype(jnp.int32)
    listing = labels.reshape(top, rows).T
    listing = listing[jax.random.permutation(jax.random.fold_in(own, 1), rows)]
    rotation = jax.random.randint(jax.random.fold_in(own, 2), (rows, 1), 0, top)
    return jnp.take_along_axis(listing, (jnp.arange(top)[None, :] + rotation) % top, axis=1)


def load_shares(count, total, reach, skew, full):
    loads = [(1 << 20) // math.isqrt(standing ** skew) + 1 for standing in range(1, count + 1)]
    largest = reach if full else min(reach, max(-(-total // count), total * loads[0] // sum(loads)))
    least = 1 if total - largest >= count - 1 else 0
    given, rest = [largest] + [least] * (count - 1), total - largest - least * (count - 1)
    while rest > 0:
        free = [i for i in range(1, count) if given[i] < largest] or [i for i in range(1, count) if given[i] < reach]
        whole, left = sum([loads[i] for i in free]), rest
        for i in free:
            extra = min(reach - given[i], max(1, left * loads[i] // whole), rest)
            given[i] = given[i] + extra
            rest = rest - extra
    return np.array(given)


def noise(own_key, dims, width, limit, split=(), kind=jnp.bfloat16):
    factor_of = levels(own_key, dims, split, -0.22, 0.18) if split else 1.0
    result = jax.random.normal(own_key, dims, jnp.float32) * width * factor_of
    return jnp.minimum(jnp.maximum(result, -limit), limit).astype(kind)


def setup_inputs(seed: int = 0) -> dict:
    keys = jax.random.split(jax.random.key(seed), 11)
    forward_acts = noise(keys[0], (N_PP, TOKENS, D), 1.0, 6.0, ((0, 8), (1, 64)))
    backward_grads = noise(keys[1], (N_PP, TOKENS, D), 1.0, 6.0, ((0, 8), (1, 64)))
    forward_routes_keys = jax.random.split(jax.random.fold_in(keys[2], 1), N_PP * TOKENS // TOK_DEV)
    forward_routes_turns = jax.random.permutation(jax.random.fold_in(keys[2], 3), N_PP * TOKENS // TOK_DEV)
    forward_routes = jax.vmap(lambda own, number: assign_block(jax.random.fold_in(keys[2], 2), own, number, TOK_DEV, EXPERTS, TOPK, ROUTE_MOST, 1))(forward_routes_keys, forward_routes_turns).reshape((N_PP, TOKENS, TOPK))
    backward_routes_keys = jax.random.split(jax.random.fold_in(keys[3], 1), N_PP * TOKENS // TOK_DEV)
    backward_routes_turns = jax.random.permutation(jax.random.fold_in(keys[3], 3), N_PP * TOKENS // TOK_DEV)
    backward_routes = jax.vmap(lambda own, number: assign_block(jax.random.fold_in(keys[3], 2), own, number, TOK_DEV, EXPERTS, TOPK, ROUTE_MOST, 1))(backward_routes_keys, backward_routes_turns).reshape((N_PP, TOKENS, TOPK))
    forward_gates = jnp.clip(0.3 + 1.2 * jax.random.uniform(keys[4], (N_PP, TOKENS, TOPK), jnp.float32) ** levels(keys[4], (N_PP, TOKENS, TOPK), ((0, 8), (1, 64)), -0.2, 0.2), 0.3, 1.5)
    backward_gates = jnp.clip(0.3 + 1.2 * jax.random.uniform(keys[5], (N_PP, TOKENS, TOPK), jnp.float32) ** levels(keys[5], (N_PP, TOKENS, TOPK), ((0, 8), (1, 64)), -0.2, 0.2), 0.3, 1.5)
    gate_weight = noise(keys[6], (N_PP, D, EXPERTS * HID), D ** -0.5, 0.09375, ((0, 8), (2, 64)))
    up_weight = noise(keys[7], (N_PP, D, EXPERTS * HID), D ** -0.5, 0.09375, ((0, 8), (2, 64)))
    down_weight = noise(keys[8], (N_PP, EXPERTS * HID, D), HID ** -0.5, 0.1875, ((0, 8), (1, 64)))
    stashed_pre = noise(keys[9], (N_PP, N_EP, N_EP, CAP, 2, HID_DEV), 1.0, 5.0, ((0, 8), (1, 64)))
    return dict(forward_acts=forward_acts, backward_grads=backward_grads, forward_routes=forward_routes, backward_routes=backward_routes, forward_gates=forward_gates, backward_gates=backward_gates, gate_weight=gate_weight, up_weight=up_weight, down_weight=down_weight, stashed_pre=stashed_pre)


def route_slots(routes):
    expert_ids = routes.reshape(N_EP, TOK_DEV * TOPK)
    columns = jnp.arange(EXPERTS, dtype=jnp.int32)
    onehot = (expert_ids[:, :, None] == columns[None, None, :]).astype(jnp.int32)
    earlier = jnp.cumsum(onehot, axis=1) - onehot
    slot_ids = jnp.sum(earlier * onehot, axis=2).astype(jnp.int32)
    return expert_ids, slot_ids


def source_index():
    device_ids = jnp.broadcast_to(jnp.arange(N_EP, dtype=jnp.int32)[:, None], (N_EP, TOK_DEV * TOPK))
    within = (jnp.arange(TOK_DEV * TOPK, dtype=jnp.int32) // TOPK).astype(jnp.int32)
    token_ids = device_ids * TOK_DEV + within[None, :]
    return device_ids, token_ids


def place_rows(values, expert_ids, device_ids, slot_ids):
    buffer = jnp.zeros((EXPERTS, N_EP, CAP, D), values.dtype)
    return buffer.at[expert_ids, device_ids, slot_ids].set(values).reshape(EXPERTS, N_EP * CAP, D)


def collect_rows(table, expert_ids, device_ids, slot_ids, weights):
    picked = table.reshape(EXPERTS, N_EP, CAP, D)[expert_ids, device_ids, slot_ids]
    picked = picked * weights[:, :, None]
    return jnp.sum(picked.reshape(N_EP * TOK_DEV, TOPK, D), axis=1)


def expert_forward(inputs):
    rows, gate_cols, up_cols, down_rows = inputs
    gate_value = jnp.dot(rows, gate_cols, preferred_element_type=jnp.float32)
    up_value = jnp.dot(rows, up_cols, preferred_element_type=jnp.float32)
    hidden = (jax.nn.silu(gate_value) * up_value).astype(jnp.bfloat16)
    hidden_blocks = hidden.astype(jnp.float32).reshape(N_EP * CAP, GROUP, HID_DEV)
    down_blocks = down_rows.astype(jnp.float32).reshape(GROUP, HID_DEV, D)
    partials = jnp.einsum('rgh,ghd->grd', hidden_blocks, down_blocks, precision=lax.Precision.HIGHEST)
    partials = lax.optimization_barrier(partials.astype(jnp.bfloat16))
    return jnp.sum(partials.astype(jnp.float32), axis=0)


def expert_backward(inputs):
    rows, stashed, gate_cols, up_cols, down_rows = inputs
    hidden_grad = jnp.dot(rows, down_rows.T, preferred_element_type=jnp.float32)
    gate_stash = stashed[:, 0, :].astype(jnp.float32)
    up_stash = stashed[:, 1, :].astype(jnp.float32)
    sigmoid_gate = jax.nn.sigmoid(gate_stash)
    gate_grad = (hidden_grad * up_stash * sigmoid_gate * (1.0 + gate_stash * (1.0 - sigmoid_gate))).astype(jnp.bfloat16)
    up_grad = (hidden_grad * gate_stash * sigmoid_gate).astype(jnp.bfloat16)
    gate_blocks = gate_grad.astype(jnp.float32).reshape(N_EP * CAP, GROUP, HID_DEV)
    up_blocks = up_grad.astype(jnp.float32).reshape(N_EP * CAP, GROUP, HID_DEV)
    gate_weights = gate_cols.astype(jnp.float32).reshape(D, GROUP, HID_DEV)
    up_weights = up_cols.astype(jnp.float32).reshape(D, GROUP, HID_DEV)
    partials = jnp.einsum('rgh,dgh->grd', gate_blocks, gate_weights, precision=lax.Precision.HIGHEST)
    partials = partials + jnp.einsum('rgh,dgh->grd', up_blocks, up_weights, precision=lax.Precision.HIGHEST)
    partials = lax.optimization_barrier(partials.astype(jnp.bfloat16))
    return jnp.sum(partials.astype(jnp.float32), axis=0)


def reference(forward_acts, backward_grads, forward_routes, backward_routes, forward_gates, backward_gates, gate_weight, up_weight, down_weight, stashed_pre):
    device_ids, token_ids = source_index()
    section_outs = []
    section_grads = []
    for section_index in range(N_PP):
        gate_cols = jnp.moveaxis(gate_weight[section_index].reshape(D, EXPERTS, HID), 1, 0)
        up_cols = jnp.moveaxis(up_weight[section_index].reshape(D, EXPERTS, HID), 1, 0)
        down_rows = down_weight[section_index].reshape(EXPERTS, HID, D)
        expert_ids, slot_ids = route_slots(forward_routes[section_index])
        acts = forward_acts[section_index]
        rows_in = place_rows(acts[token_ids], expert_ids, device_ids, slot_ids)
        out_fwd = lax.map(expert_forward, (rows_in, gate_cols, up_cols, down_rows))
        weights = forward_gates[section_index].reshape(N_EP, TOK_DEV * TOPK)
        routed = collect_rows(out_fwd, expert_ids, device_ids, slot_ids, weights)
        section_outs.append((acts.astype(jnp.float32) + routed).astype(jnp.bfloat16))
        back_ids, back_slots = route_slots(backward_routes[section_index])
        grads = backward_grads[section_index]
        back_weights = backward_gates[section_index].reshape(N_EP, TOK_DEV * TOPK)
        scaled = (back_weights[:, :, None] * grads[token_ids].astype(jnp.float32)).astype(jnp.bfloat16)
        cot_in = place_rows(scaled, back_ids, device_ids, back_slots)
        stashed = stashed_pre[section_index].reshape(EXPERTS, GROUP, N_EP, CAP, 2, HID_DEV)
        stashed = jnp.transpose(stashed, (0, 2, 3, 4, 1, 5)).reshape(EXPERTS, N_EP * CAP, 2, HID)
        out_bwd = lax.map(expert_backward, (cot_in, stashed, gate_cols, up_cols, down_rows))
        unit = jnp.ones((N_EP, TOK_DEV * TOPK), jnp.float32)
        returned = collect_rows(out_bwd, back_ids, device_ids, back_slots, unit)
        section_grads.append((grads.astype(jnp.float32) + returned).astype(jnp.bfloat16))
    forward_next = jnp.roll(jnp.stack(section_outs), -1, axis=0)
    backward_next = jnp.roll(jnp.stack(section_grads), -1, axis=0)
    return forward_next, backward_next
```

```python
import functools

import jax
import jax.numpy as jnp
from jax import lax
from jax.experimental import pallas as pl
from jax.experimental.pallas import tpu as pltpu
from jax.sharding import PartitionSpec as P

MESH = pl.DeviceIdType.MESH
BF = jnp.bfloat16
F32 = jnp.float32
TOK = 24
CAP = 8
PAIR = 16
NZ = 8
NY = 4
SLOTS = NZ * PAIR
TILE = 512
ORDER = (0, 1, 7, 2, 6, 3, 5, 4)
N_SEM = 208


def slot_table(routes, gates, shift, core):
    place = lax.broadcasted_iota(jnp.int32, (TOK, SLOTS), 1)
    expert = ((place >> 4) + shift) & 7
    mine = ((place >> 3) & 1) == core
    number = (place & 7).astype(F32)
    first = routes[:, 0:1] == expert
    second = routes[:, 1:2] == expert
    named = jnp.where(first | second, 1.0, 0.0).astype(BF)
    row = lax.broadcasted_iota(jnp.int32, (TOK, TOK), 0)
    col = lax.broadcasted_iota(jnp.int32, (TOK, TOK), 1)
    before = jnp.where(col < row, 1.0, 0.0).astype(BF)
    earlier = jnp.dot(before, named, preferred_element_type=F32)
    here = (earlier == number) & mine
    return jnp.where(here & first, gates[:, 0:1], 0.0) + jnp.where(here & second, gates[:, 1:2], 0.0)


def split(table):
    high = table.astype(BF)
    return high, (table - high.astype(F32)).astype(BF)


def plain(table):
    return jnp.where(table > 0.0, 1.0, 0.0).astype(BF)


def lead(a, b):
    return lax.dot_general(a, b, (((0,), (0,)), ((), ())), preferred_element_type=F32)


def trail(a, b):
    return lax.dot_general(a, b, (((1,), (1,)), ((), ())), preferred_element_type=F32)


def dot(a, b):
    return jnp.dot(a, b, preferred_element_type=F32)


def kernel(
    acts, grads, routes_f, routes_b, gates_f, gates_b, w_gate, w_up, w_down, stash,
    out_f, out_b,
    rows, part, back, slots, toks, tabs, sums, gets, wgu, wd, st, acc,
    send_sem, recv_sem, local_sem,
):
    width = rows.shape[2]
    tiles = width // TILE
    pp, ep = lax.axis_index("pp"), lax.axis_index("ep")
    n_pp = lax.axis_size("pp")
    z, y, core = ep // 8, lax.rem(ep, 8) // 2, lax.rem(ep, 2)
    pp_next = lax.rem(pp + n_pp - 1, n_pp)
    pp_prev = lax.rem(pp + 1, n_pp)

    def at_z(d):
        return lax.rem(z + d + NZ, NZ)

    def at_y(r):
        return lax.rem(y + r + NY, NY)

    def dev(d, r, c, section=None):
        return (pp if section is None else section, at_z(d) * 8 + at_y(r) * 2 + c)

    partner = dev(0, 0, 1 - core)

    ids, started, locals_ = {}, [], []

    def sem_of(key):
        return ids.setdefault(key, len(ids))

    def send(key, src, dst, target, lane=0):
        copy = pltpu.make_async_remote_copy(
            src_ref=src, dst_ref=dst, send_sem=send_sem.at[sem_of((key, lane) if lane else key)],
            recv_sem=recv_sem.at[sem_of(key)], device_id=target, device_id_type=MESH,
        )
        copy.start()
        started.append(copy)

    def arrive(key, dst):
        pltpu.make_async_remote_copy(
            src_ref=dst, dst_ref=dst, send_sem=send_sem.at[sem_of(key)],
            recv_sem=recv_sem.at[sem_of(key)], device_id=partner, device_id_type=MESH,
        ).wait_recv()

    def sent():
        for copy in started:
            copy.wait_send()
        started.clear()

    def local(src, dst):
        copy = pltpu.make_async_copy(src, dst, local_sem.at[len(locals_)])
        locals_.append(copy)
        copy.start()
        return copy

    def tiled(step):
        lax.fori_loop(0, tiles, lambda i, _: (step(pl.ds(pl.multiple_of(i * TILE, TILE), TILE)), 0)[1], 0)

    barrier = pltpu.get_barrier_semaphore()

    def greet(target):
        pl.semaphore_signal(barrier, inc=1, device_id=target, device_id_type=MESH)

    greet(partner)
    for d in range(1, NZ):
        greet(dev(d, 0, core))
    for r in (1, 3):
        greet(dev(0, r, core))
    greet(dev(0, 0, 0, pp_prev))
    for r in range(NY):
        greet(dev(0, r, 1, pp_prev))

    def load_weights(c):
        cols = pl.ds(c * 128, 128)
        ups = pl.ds((2 + c) * 128, 128)
        return [
            local(w_gate.at[0], wgu.at[:, cols]),
            local(w_up.at[0], wgu.at[:, ups]),
            local(w_down.at[0], wd.at[pl.ds(c * 128, 128)]),
        ]

    def send_weights(c):
        send(("gate", c), w_gate.at[0], wgu.at[:, pl.ds(c * 128, 128)], partner)
        send(("up", c), w_up.at[0], wgu.at[:, pl.ds((2 + c) * 128, 128)], partner)
        send(("down", c), w_down.at[0], wd.at[pl.ds(c * 128, 128)], partner)

    def get_weights(c):
        arrive(("gate", c), wgu.at[:, pl.ds(c * 128, 128)])
        arrive(("up", c), wgu.at[:, pl.ds((2 + c) * 128, 128)])
        arrive(("down", c), wd.at[pl.ds(c * 128, 128)])

    def build(base, r, tables, weighted):
        left = []
        for c in (0, 1):
            left.append(split(tables[c]) if weighted else (plain(tables[c]),))

        def step(cols):
            total = None
            for c in (0, 1):
                for one in left[c]:
                    term = lead(one, toks[r, c, :, cols])
                    total = term if total is None else total + term
            slots[pl.ds(base, NZ), :, cols] = total.astype(BF).reshape(NZ, PAIR, TILE)

        tiled(step)

    @pl.when(core == 0)
    def forward():
        near = local(acts.at[0], toks.at[0, 0])
        mine = load_weights(0)
        tabs[0, 0] = slot_table(routes_f[...], gates_f[...], z, 0)
        tabs[4, 0] = slot_table(routes_b[...], gates_b[...], 0, 0)
        pl.semaphore_wait(barrier, 12)
        send("grads", grads.at[0], toks.at[0, 0], partner)
        send("tab_b", tabs.at[4, 0], tabs.at[0, 0], partner)
        send("stash", stash, st.at[0], partner)
        send_weights(0)
        near.wait()
        arrive("acts", toks.at[0, 1])
        arrive("tab_f", tabs.at[0, 1])

        build(0, 0, (tabs[0, 0], tabs[0, 1]), False)

        def row(r, i):
            return (i // 4) * 16 + r * 4 + i % 4

        for i in range(1, NZ):
            d = ORDER[i]
            send(("zf", i), slots.at[d], rows.at[row(0, i)], dev(d, 0, 0))
        own = local(slots.at[0], rows.at[row(0, 0)])

        def spread(i):
            if i:
                arrive(("zf", i), rows.at[row(0, i)])
            source = rows.at[row(0, i)] if i else slots.at[0]
            send(("yp", i), source, rows.at[row(1, i)], dev(0, 1, 0))
            send(("ym", i), source, rows.at[row(3, i)], dev(0, 3, 0))

        def relay(i):
            arrive(("yp", i), rows.at[row(1, i)])
            arrive(("ym", i), rows.at[row(3, i)])
            if i % 2 == 0:
                send(("yy", i), rows.at[row(1, i)], rows.at[row(2, i)], dev(0, 1, 0))
            else:
                send(("yy", i), rows.at[row(3, i)], rows.at[row(2, i)], dev(0, 3, 0))

        def compute(h):
            for i in range(4 * h, 4 * h + 4):
                arrive(("yy", i), rows.at[row(2, i)])
            whole = pl.ds(16 * h, 16)
            acc[...] = jnp.zeros_like(acc)

            def one(cols):
                acc[...] += dot(rows[whole, :, cols].reshape(256, TILE), wgu[cols, :])

            tiled(one)
            gate, up = acc[:, :256], acc[:, 256:]
            hidden = (gate * jax.nn.sigmoid(gate) * up).astype(BF)

            def two(cols):
                part[whole, :, cols] = dot(hidden, wd[:, cols]).astype(BF).reshape(16, PAIR, TILE)

            tiled(two)

        def reduce_first(h):
            b = 16 * h
            q = 12 * h
            send(("rp", h), part.at[pl.ds(b + 8, 2)], back.at[pl.ds(q, 2)], dev(0, 1, 0))
            send(("rm", h), part.at[pl.ds(b + 10, 2)], back.at[pl.ds(q + 2, 2)], dev(0, 3, 0))
            send(("sp", h, 1), part.at[pl.ds(b + 14, 2)], back.at[pl.ds(q + 6, 2)], dev(0, 1, 0))
            send(("sm", h, 0), part.at[pl.ds(b + 4, 2)], back.at[pl.ds(q + 8, 2)], dev(0, 3, 0))

        def reduce_second(h):
            b = 16 * h
            q = 12 * h
            arrive(("rp", h), back.at[pl.ds(q, 2)])
            total = part[pl.ds(b + 12, 2)].astype(F32) + back[pl.ds(q, 2)].astype(F32)
            part[pl.ds(b + 12, 2)] = total.astype(BF)
            send(("sp", h, 0), part.at[pl.ds(b + 12, 2)], back.at[pl.ds(q + 4, 2)], dev(0, 1, 0))
            arrive(("rm", h), back.at[pl.ds(q + 2, 2)])
            total = part[pl.ds(b + 6, 2)].astype(F32) + back[pl.ds(q + 2, 2)].astype(F32)
            part[pl.ds(b + 6, 2)] = total.astype(BF)
            send(("sm", h, 1), part.at[pl.ds(b + 6, 2)], back.at[pl.ds(q + 10, 2)], dev(0, 3, 0))

        def reduce_last(h):
            b = 16 * h
            q = 12 * h
            arrive(("sp", h, 0), back.at[pl.ds(q + 4, 2)])
            arrive(("sp", h, 1), back.at[pl.ds(q + 6, 2)])
            arrive(("sm", h, 0), back.at[pl.ds(q + 8, 2)])
            arrive(("sm", h, 1), back.at[pl.ds(q + 10, 2)])
            for j in range(4):
                d = ORDER[4 * h + j]
                total = (
                    part[b + j].astype(F32) + back[q + 4 + j].astype(F32) + back[q + 8 + j].astype(F32)
                ).astype(BF)
                if d == 0:
                    back[24] = total
                else:
                    slots[8 + d] = total
                    send(("zr", d), slots.at[8 + d], back.at[24 + d], dev(-d, 0, 0))

        for i in range(4):
            spread(i)
            if i:
                relay(i - 1)
        relay(3)
        for i in range(4, 8):
            spread(i)
        own.wait()
        for copy in mine:
            copy.wait()
        get_weights(1)
        compute(0)
        for i in range(4, 8):
            relay(i)
        reduce_first(0)
        reduce_second(0)
        compute(1)
        reduce_first(1)
        reduce_last(0)
        reduce_second(1)
        reduce_last(1)
        for d in range(1, NZ):
            arrive(("zr", d), back.at[24 + d])
        for c in (0, 1):
            high, low = split(tabs[0, c])

            def step(cols):
                got = back[pl.ds(24, NZ), :, cols].reshape(SLOTS, TILE)
                total = toks[0, c, :, cols].astype(F32) + dot(high, got) + dot(low, got)
                sums[0, c, :, cols] = total.astype(BF)

            tiled(step)
            send(("out", 0), sums.at[0, c], out_f.at[0], dev(0, 0, c, pp_next), c)
        sent()

    locals_.clear()

    @pl.when(core == 1)
    def backward():
        mine = load_weights(1)
        near = local(grads.at[0], toks.at[0, 1])
        keep = local(stash, st.at[1])
        tabs[0, 1] = slot_table(routes_b[...], gates_b[...], 0, 1)
        tabs[4, 1] = slot_table(routes_f[...], gates_f[...], z, 1)
        pl.semaphore_wait(barrier, 18)
        send("acts", acts.at[0], toks.at[0, 1], partner)
        send("tab_f", tabs.at[4, 1], tabs.at[0, 1], partner)
        send(("tp", 1), grads.at[0], toks.at[1, 1], dev(0, 1, 1))
        send(("tm", 1), grads.at[0], toks.at[3, 1], dev(0, 3, 1))
        send_weights(1)
        arrive("grads", toks.at[0, 0])
        arrive("tab_b", tabs.at[0, 0])
        send(("tp", 0), toks.at[0, 0], toks.at[1, 0], dev(0, 1, 1))
        send(("tm", 0), toks.at[0, 0], toks.at[3, 0], dev(0, 3, 1))
        send("tabp", tabs.at[0], tabs.at[1], dev(0, 1, 1))
        send("tabm", tabs.at[0], tabs.at[2], dev(0, 3, 1))
        near.wait()
        own = []

        table_at = (0, 1, 3, 2)

        def scatter(r):
            build(8 * r, r, (tabs[table_at[r], 0], tabs[table_at[r], 1]), True)
            own.append(local(slots.at[8 * r + z], rows.at[8 * r + z]))
            for d in ORDER[1:]:
                send(("c", r, d), slots.at[8 * r + at_z(d)], rows.at[8 * r + z], dev(d, 0, 1))

        scatter(0)
        arrive(("tp", 0), toks.at[1, 0])
        arrive(("tp", 1), toks.at[1, 1])
        arrive("tabp", tabs.at[1])
        send(("ty", 0), toks.at[1, 0], toks.at[2, 0], dev(0, 1, 1))
        send("taby", tabs.at[1], tabs.at[3], dev(0, 1, 1))
        arrive(("tm", 0), toks.at[3, 0])
        arrive(("tm", 1), toks.at[3, 1])
        arrive("tabm", tabs.at[2])
        send(("ty", 1), toks.at[3, 1], toks.at[2, 1], dev(0, 3, 1))
        scatter(1)
        scatter(3)
        arrive(("ty", 0), toks.at[2, 0])
        arrive(("ty", 1), toks.at[2, 1])
        arrive("taby", tabs.at[3])
        scatter(2)

        for copy in mine:
            copy.wait()
        keep.wait()
        get_weights(0)
        arrive("stash", st.at[0])
        pick_row = lax.broadcasted_iota(jnp.int32, (SLOTS, 2 * SLOTS), 0)
        pick_col = lax.broadcasted_iota(jnp.int32, (SLOTS, 2 * SLOTS), 1)
        even = jnp.where(pick_col == 2 * pick_row, 1.0, 0.0).astype(BF)
        odd = jnp.where(pick_col == 2 * pick_row + 1, 1.0, 0.0).astype(BF)

        def compute(r, own_copy):
            own_copy.wait()
            for d in ORDER[1:]:
                arrive(("c", r, d), rows.at[8 * r + at_z(-d)])
            whole = pl.ds(8 * r, NZ)
            acc[0:SLOTS, 0:256] = jnp.zeros((SLOTS, 256), F32)

            def one(cols):
                acc[0:SLOTS, 0:256] += trail(rows[whole, :, cols].reshape(SLOTS, TILE), wd[:, cols])

            tiled(one)
            grad = []
            for c in (0, 1):
                both = st[c, :, at_y(-r)].reshape(2 * SLOTS, 128)
                gate, up = dot(even, both), dot(odd, both)
                q = jax.nn.sigmoid(gate)
                hidden = acc[0:SLOTS, 128 * c : 128 * c + 128]
                grad.append(
                    (
                        (hidden * up * q * (1.0 + gate * (1.0 - q))).astype(BF),
                        (hidden * gate * q).astype(BF),
                    )
                )
            both = jnp.concatenate([grad[0][0], grad[1][0], grad[0][1], grad[1][1]], axis=1)

            def two(cols):
                part[whole, :, cols] = trail(both, wgu[cols, :]).astype(BF).reshape(NZ, PAIR, TILE)

            tiled(two)
            own.append(local(part.at[8 * r + z], back.at[8 * r + z]))
            for d in ORDER[1:]:
                send(("p", r, d), part.at[8 * r + at_z(-d)], back.at[8 * r + z], dev(-d, 0, 1))

        def combine(r, own_copy):
            own_copy.wait()
            for d in ORDER[1:]:
                arrive(("p", r, d), back.at[8 * r + at_z(d)])
            for c in (0, 1):
                table = plain(tabs[table_at[r], c])

                def step(cols):
                    total = dot(table, back[pl.ds(8 * r, NZ), :, cols].reshape(SLOTS, TILE))
                    if r == 0:
                        total = total + toks[0, c, :, cols].astype(F32)
                    sums[r, c, :, cols] = total.astype(BF)

                tiled(step)
                send(("end", r), sums.at[r, c], gets.at[r], dev(0, -r, c, pp_next), c)

        order = (0, 1, 3, 2)
        for n, r in enumerate(order):
            compute(r, own[n])
        for n, r in enumerate(order):
            combine(r, own[4 + n])
        sent()

    for r in (0, 1, 3, 2):
        arrive(("end", r), gets.at[r])

    def total(cols):
        out_b[0, :, cols] = (
            gets[0, :, cols].astype(F32)
            + gets[1, :, cols].astype(F32)
            + gets[2, :, cols].astype(F32)
            + gets[3, :, cols].astype(F32)
        ).astype(BF)

    tiled(total)
    arrive(("out", 0), out_f.at[0])
    assert len(ids) <= N_SEM


def on_device(acts, grads, routes_f, routes_b, gates_f, gates_b, w_gate, w_up, w_down, stash):
    width = acts.shape[2]
    anywhere = pl.BlockSpec(memory_space=pl.ANY)
    inside = pl.BlockSpec(memory_space=pltpu.VMEM)
    out = jax.ShapeDtypeStruct((1, TOK, width), BF)
    chunks = pltpu.VMEM((NZ * NY, PAIR, width), BF)
    return pl.pallas_call(
        kernel,
        name="relay",
        out_shape=(out, out),
        in_specs=[anywhere, anywhere, inside, inside, inside, inside] + [anywhere] * 4,
        out_specs=(anywhere, inside),
        scratch_shapes=[
            chunks,
            chunks,
            chunks,
            chunks,
            pltpu.VMEM((NY, 2, TOK, width), BF),
            pltpu.VMEM((5, 2, TOK, SLOTS), F32),
            pltpu.VMEM((NY, 2, TOK, width), BF),
            pltpu.VMEM((NY, TOK, width), BF),
            pltpu.VMEM((width, 512), BF),
            pltpu.VMEM((256, width), BF),
            pltpu.VMEM((2, NZ, NY, 32, 128), BF),
            pltpu.VMEM((256, 512), F32),
            pltpu.SemaphoreType.DMA((N_SEM,)),
            pltpu.SemaphoreType.DMA((N_SEM,)),
            pltpu.SemaphoreType.DMA((16,)),
        ],
        compiler_params=pltpu.CompilerParams(
            collective_id=0, has_side_effects=True, vmem_limit_bytes=56 * 2**20
        ),
    )(
        acts, grads, routes_f[0], routes_b[0], gates_f[0], gates_b[0],
        w_gate, w_up, w_down, stash.reshape(NZ, NY, 32, 128),
    )


def solution(mesh):
    placed = (
        P("pp", "ep", None),
        P("pp", "ep", None),
        P("pp", "ep", None),
        P("pp", "ep", None),
        P("pp", "ep", None),
        P("pp", "ep", None),
        P("pp", None, "ep"),
        P("pp", None, "ep"),
        P("pp", "ep", None),
        P("pp", "ep", None, None, None, None),
    )
    return jax.shard_map(
        on_device,
        mesh=mesh,
        in_specs=placed,
        out_specs=(P("pp", "ep", None), P("pp", "ep", None)),
        check_vma=False,
    )
```

```python
import functools

import jax
import jax.numpy as jnp
from jax import lax
from jax.experimental import pallas as pl
from jax.experimental.pallas import tpu as pltpu
from jax.sharding import PartitionSpec as P

MESH = pl.DeviceIdType.MESH
BF = jnp.bfloat16
F32 = jnp.float32
TOK = 24
CAP = 8
PAIR = 16
NZ = 8
NY = 4
SLOTS = NZ * PAIR
TILE = 512
ORDER = (0, 1, 7, 2, 6, 3, 5, 4)
CLOSE = ORDER[1:7]
APART = ORDER[7:]
LAG = 2
GATE = 3
FLOW = ("mid", "near", "far", "own")
N_SEM = 208


def slot_table(routes, gates, shift, core):
    place = lax.broadcasted_iota(jnp.int32, (SLOTS, TOK), 0)
    expert = ((place >> 4) + shift) & 7
    mine = ((place >> 3) & 1) == core
    number = (place & 7).astype(F32)
    first = routes[0:1, :] == expert
    second = routes[1:2, :] == expert
    named = jnp.where(first | second, 1.0, 0.0).astype(BF)
    row = lax.broadcasted_iota(jnp.int32, (TOK, TOK), 0)
    col = lax.broadcasted_iota(jnp.int32, (TOK, TOK), 1)
    before = jnp.where(row < col, 1.0, 0.0).astype(BF)
    earlier = dot(named, before)
    here = (earlier == number) & mine
    return jnp.where(here & first, gates[0:1, :], 0.0) + jnp.where(here & second, gates[1:2, :], 0.0)


def split(table):
    high = table.astype(BF)
    return high, (table - high.astype(F32)).astype(BF)


def plain(table):
    return jnp.where(table > 0.0, 1.0, 0.0).astype(BF)


def lead(a, b):
    return lax.dot_general(a, b, (((0,), (0,)), ((), ())), preferred_element_type=F32)


def trail(a, b):
    return lax.dot_general(a, b, (((1,), (1,)), ((), ())), preferred_element_type=F32)


def dot(a, b):
    return jnp.dot(a, b, preferred_element_type=F32)


def kernel(
    acts, grads, routes_f, routes_b, gates_f, gates_b, w_gate, w_up, w_down, stash,
    out_f, out_b,
    rows, part, back, slots, toks, named, scale, sums, gets, wgu, wd, st, acc,
    send_sem, recv_sem, local_sem, go,
):
    width = rows.shape[2]
    tiles = width // TILE
    pp, ep = lax.axis_index("pp"), lax.axis_index("ep")
    n_pp = lax.axis_size("pp")
    z, y, core = ep // 8, lax.rem(ep, 8) // 2, lax.rem(ep, 2)
    pp_next = lax.rem(pp + n_pp - 1, n_pp)
    pp_prev = lax.rem(pp + 1, n_pp)
    side = 2 * lax.rem(pp, 2) - 1
    mid, near = 2 - side, 2 + side

    def at_z(d):
        return lax.rem(z + d + NZ, NZ)

    def at_y(r):
        return lax.rem(y + r + NY, NY)

    def dev(d, r, c, section=None):
        return (pp if section is None else section, at_z(d) * 8 + at_y(r) * 2 + c)

    partner = dev(0, 0, 1 - core)

    ids, started, locals_ = {}, [], []

    def sem_of(key):
        return ids.setdefault(key, len(ids))

    def send(key, src, dst, target, lane=0):
        copy = pltpu.make_async_remote_copy(
            src_ref=src, dst_ref=dst, send_sem=send_sem.at[sem_of((key, lane) if lane else key)],
            recv_sem=recv_sem.at[sem_of(key)], device_id=target, device_id_type=MESH,
        )
        copy.start()
        started.append(copy)

    def arrive(key, dst):
        pltpu.make_async_remote_copy(
            src_ref=dst, dst_ref=dst, send_sem=send_sem.at[sem_of(key)],
            recv_sem=recv_sem.at[sem_of(key)], device_id=partner, device_id_type=MESH,
        ).wait_recv()

    def sent():
        for copy in started:
            copy.wait_send()
        started.clear()

    def local(src, dst):
        copy = pltpu.make_async_copy(src, dst, local_sem.at[len(locals_)])
        locals_.append(copy)
        copy.start()
        return copy

    def tiled(step):
        lax.fori_loop(0, tiles, lambda i, _: (step(pl.ds(pl.multiple_of(i * TILE, TILE), TILE)), 0)[1], 0)

    barrier = pltpu.get_barrier_semaphore()

    def greet(target):
        pl.semaphore_signal(barrier, inc=1, device_id=target, device_id_type=MESH)

    greet(partner)
    for d in range(1, NZ):
        greet(dev(d, 0, core))
    for r in (1, 3):
        greet(dev(0, r, core))
    greet(dev(0, 0, 1, pp_prev))
    greet(dev(0, side, 1, pp_prev))

    @pl.when(core == 0)
    def others():
        greet(dev(0, 0, 0, pp_prev))
        greet(dev(0, side, 0, pp_prev))

    @pl.when(core == 1)
    def across():
        greet(dev(0, 2, 1))

    def load_weights(c):
        cols = pl.ds(c * 128, 128)
        ups = pl.ds((2 + c) * 128, 128)
        return [
            local(w_gate.at[0], wgu.at[:, cols]),
            local(w_up.at[0], wgu.at[:, ups]),
            local(w_down.at[0], wd.at[pl.ds(c * 128, 128)]),
        ]

    def send_weights(c):
        send(("gate", c), w_gate.at[0], wgu.at[:, pl.ds(c * 128, 128)], partner)
        send(("up", c), w_up.at[0], wgu.at[:, pl.ds((2 + c) * 128, 128)], partner)
        send(("down", c), w_down.at[0], wd.at[pl.ds(c * 128, 128)], partner)

    def get_weights(c):
        arrive(("gate", c), wgu.at[:, pl.ds(c * 128, 128)])
        arrive(("up", c), wgu.at[:, pl.ds((2 + c) * 128, 128)])
        arrive(("down", c), wd.at[pl.ds(c * 128, 128)])

    def build(base, r, tables, weighted):
        left = []
        for c in (0, 1):
            left.append(split(tables[c]) if weighted else (plain(tables[c]),))

        def step(cols):
            total = None
            for c in (0, 1):
                for one in left[c]:
                    term = dot(one, toks[r, c, :, cols])
                    total = term if total is None else total + term
            slots[pl.ds(base, NZ), :, cols] = total.astype(BF).reshape(NZ, PAIR, TILE)

        tiled(step)

    @pl.when(core == 0)
    def forward():
        waits = [
            local(acts.at[0], toks.at[0, 0]),
            local(routes_f, named.at[0, 0]),
            local(gates_f, scale.at[0, 0]),
        ]
        mine = load_weights(0)
        pl.semaphore_wait(barrier, 12)
        send("routes_b", routes_b, named.at[0, 0], partner)
        send("gates_b", gates_b, scale.at[0, 0], partner)
        send("grads", grads.at[0], toks.at[0, 0], partner)
        send(("nextn", 0), routes_f, named.at[1, 0], dev(0, 0, 0, pp_next))
        send(("nexts", 0), gates_f, scale.at[1, 0], dev(0, 0, 0, pp_next))
        for copy in waits:
            copy.wait()
        arrive("routes_f", named.at[0, 1])
        arrive("gates_f", scale.at[0, 1])
        tables = [slot_table(named[0, c], scale[0, c], z, c) for c in (0, 1)]
        arrive("acts", toks.at[0, 1])

        build(0, 0, tables, False)

        def row(r, i):
            return (i // 4) * 16 + r * 4 + i % 4

        for i in range(1, NZ):
            d = ORDER[i]
            send(("zf", i), slots.at[d], rows.at[row(0, i)], dev(d, 0, 0))
        own = local(slots.at[0], rows.at[row(0, 0)])

        def spread(i):
            if i:
                arrive(("zf", i), rows.at[row(0, i)])
            if i == GATE:
                pl.semaphore_signal(go, inc=1, device_id=partner, device_id_type=MESH)
            source = rows.at[row(0, i)] if i else slots.at[0]
            send(("yp", i), source, rows.at[row(1, i)], dev(0, 1, 0))
            send(("ym", i), source, rows.at[row(3, i)], dev(0, 3, 0))

        def relay(i):
            arrive(("yp", i), rows.at[row(1, i)])
            arrive(("ym", i), rows.at[row(3, i)])
            if i % 2 == 0:
                send(("yy", i), rows.at[row(1, i)], rows.at[row(2, i)], dev(0, 1, 0))
            else:
                send(("yy", i), rows.at[row(3, i)], rows.at[row(2, i)], dev(0, 3, 0))

        def compute(h):
            for i in range(4 * h, 4 * h + 4):
                arrive(("yy", i), rows.at[row(2, i)])
            whole = pl.ds(16 * h, 16)
            acc[...] = jnp.zeros_like(acc)

            def one(cols):
                acc[...] += dot(rows[whole, :, cols].reshape(256, TILE), wgu[cols, :])

            tiled(one)
            gate, up = acc[:, :256], acc[:, 256:]
            hidden = (gate * jax.nn.sigmoid(gate) * up).astype(BF)

            def two(cols):
                part[whole, :, cols] = dot(hidden, wd[:, cols]).astype(BF).reshape(16, PAIR, TILE)

            tiled(two)

        def spot(g, r):
            return pl.ds(16 * (g // 2) + 2 * (g % 2) + 4 * r, 2)

        def land(g, n):
            return pl.ds(8 * g + 2 * n, 2)

        def reduce_first(g):
            send(("r2", g), part.at[spot(g, 2)], back.at[land(g, 0)], dev(0, side, 0))
            send(("rm", g), part.at[spot(g, mid)], back.at[land(g, 1)], dev(0, -side, 0))

        def reduce_second(g):
            for name, n, r, target in (("r2", 0, near, side), ("rm", 1, 0, 0)):
                arrive((name, g), back.at[land(g, n)])

                def add(cols):
                    total = part[spot(g, r), :, cols].astype(F32) + back[land(g, n), :, cols].astype(F32)
                    part[spot(g, r), :, cols] = total.astype(BF)

                tiled(add)
                send(("s" + name, g), part.at[spot(g, r)], back.at[land(g, 2 + n)], dev(0, target, 0, pp_next))

        def reduce_last(g):
            arrive(("sr2", g), back.at[land(g, 2)])
            arrive(("srm", g), back.at[land(g, 3)])
            for j in (1, 0):
                d = ORDER[2 * g + j]
                place = 16 if d == 0 else 8 + d

                def add(cols):
                    total = back[8 * g + 4 + j, :, cols].astype(F32) + back[8 * g + 6 + j, :, cols].astype(F32)
                    slots[place, :, cols] = total.astype(BF)

                tiled(add)
                if d:
                    send(("zr", d), slots.at[8 + d], slots.at[16 + d], dev(-d, 0, 0))

        for i in range(LAG):
            spread(i)
        send("stash", stash, st.at[0], partner)
        send_weights(0)
        for i in range(4):
            spread(i + LAG)
            relay(i)
        for i in range(4 + LAG, NZ):
            spread(i)
        send(("next", 0), acts.at[0], toks.at[1, 0], dev(0, 0, 0, pp_next))
        own.wait()
        for copy in mine:
            copy.wait()
        get_weights(1)
        compute(0)
        for i in range(4, 8):
            relay(i)
        reduce_first(0)
        reduce_first(1)
        compute(1)
        reduce_second(0)
        reduce_second(1)
        reduce_first(2)
        reduce_first(3)
        reduce_last(0)
        reduce_second(2)
        reduce_last(1)
        reduce_second(3)
        reduce_last(2)
        reduce_last(3)
        for c in (0, 1):
            arrive(("next", c), toks.at[1, c])
            arrive(("nextn", c), named.at[1, c])
            arrive(("nexts", c), scale.at[1, c])
        left = [split(slot_table(named[1, c], scale[1, c], z, c)) for c in (0, 1)]
        for d in range(1, NZ):
            arrive(("zr", d), slots.at[16 + d])
        for c in (1, 0):
            high, low = left[c]

            def step(cols):
                got = slots[pl.ds(16, NZ), :, cols].reshape(SLOTS, TILE)
                total = toks[1, c, :, cols].astype(F32) + lead(high, got) + lead(low, got)
                sums[0, c, :, cols] = total.astype(BF)

            tiled(step)
            if c:
                send("out", sums.at[0, 1], out_f.at[0], partner)
            else:
                last = local(sums.at[0, 0], out_f.at[0])
        last.wait()
        sent()

    locals_.clear()

    @pl.when(core == 1)
    def backward():
        waits = [
            local(grads.at[0], toks.at[0, 1]),
            local(routes_b, named.at[0, 1]),
            local(gates_b, scale.at[0, 1]),
        ]
        keep = local(stash, st.at[1])
        mine = load_weights(1)
        pl.semaphore_wait(barrier, 15)
        send("routes_f", routes_f, named.at[0, 1], partner)
        send("gates_f", gates_f, scale.at[0, 1], partner)
        send("acts", acts.at[0], toks.at[0, 1], partner)
        send(("tm", 1), grads.at[0], toks.at[mid, 1], dev(0, side, 1))
        send(("tn", 1), grads.at[0], toks.at[near, 1], dev(0, -side, 1))
        for copy in waits:
            copy.wait()
        arrive("routes_b", named.at[0, 0])
        arrive("gates_b", scale.at[0, 0])
        for name, r, target in (("mid", mid, side), ("near", near, -side), ("far", 2, 2)):
            send(("nr", name), named.at[0], named.at[r], dev(0, target, 1))
            send(("ng", name), scale.at[0], scale.at[r], dev(0, target, 1))
        arrive("grads", toks.at[0, 0])
        send(("tm", 0), toks.at[0, 0], toks.at[mid, 0], dev(0, side, 1))
        send(("tn", 0), toks.at[0, 0], toks.at[near, 0], dev(0, -side, 1))
        own = {}
        index = {"own": 0, "mid": mid, "near": near, "far": 2}

        def tables(r):
            return [slot_table(named[r, c], scale[r, c], 0, c) for c in (0, 1)]

        def scatter(name):
            r = index[name]
            if name != "own":
                arrive(("nr", name), named.at[r])
                arrive(("ng", name), scale.at[r])
            build(8 * r, r, tables(r), True)
            own[name] = local(slots.at[8 * r + z], rows.at[8 * r + z])
            if name == "own" and GATE >= 0:
                pl.semaphore_wait(go, 1)
            for d in (APART + CLOSE if name == "own" else CLOSE):
                send(("c", name, d), slots.at[8 * r + at_z(d)], rows.at[8 * r + z], dev(d, 0, 1))

        scatter("own")
        send_weights(1)
        arrive(("tm", 0), toks.at[mid, 0])
        arrive(("tm", 1), toks.at[mid, 1])
        send(("ty", 0), toks.at[mid, 0], toks.at[2, 0], dev(0, side, 1))
        arrive(("tn", 0), toks.at[near, 0])
        arrive(("tn", 1), toks.at[near, 1])
        send(("ty", 1), toks.at[near, 1], toks.at[2, 1], dev(0, -side, 1))
        send(("next", 1), acts.at[0], toks.at[1, 1], dev(0, 0, 0, pp_next))
        send(("nextn", 1), routes_f, named.at[1, 1], dev(0, 0, 0, pp_next))
        send(("nexts", 1), gates_f, scale.at[1, 1], dev(0, 0, 0, pp_next))
        scatter("mid")
        scatter("near")
        arrive(("ty", 0), toks.at[2, 0])
        arrive(("ty", 1), toks.at[2, 1])
        scatter("far")

        half = pl.ds(0, width // 2)
        rest = pl.ds(width // 2, width // 2)
        for d in APART:
            source = at_z(-d)
            arrive(("c", "own", d), rows.at[source])
            send(("fp", d), rows.at[source], rows.at[8 * mid + source], dev(0, side, 1))
            send(("fm", d), rows.at[source], rows.at[8 * near + source], dev(0, -side, 1))
        for d in APART:
            source = at_z(-d)
            arrive(("fp", d), rows.at[8 * mid + source])
            send(("fy", 0, d), rows.at[8 * mid + source, :, half], rows.at[16 + source, :, half], dev(0, side, 1))
            arrive(("fm", d), rows.at[8 * near + source])
            send(("fy", 1, d), rows.at[8 * near + source, :, rest], rows.at[16 + source, :, rest], dev(0, -side, 1))

        for copy in mine:
            copy.wait()
        keep.wait()
        get_weights(0)
        arrive("stash", st.at[0])
        pick_row = lax.broadcasted_iota(jnp.int32, (SLOTS, 2 * SLOTS), 0)
        pick_col = lax.broadcasted_iota(jnp.int32, (SLOTS, 2 * SLOTS), 1)
        even = jnp.where(pick_col == 2 * pick_row, 1.0, 0.0).astype(BF)
        odd = jnp.where(pick_col == 2 * pick_row + 1, 1.0, 0.0).astype(BF)

        def compute(name):
            r = index[name]
            own[name].wait()
            for d in CLOSE:
                arrive(("c", name, d), rows.at[8 * r + at_z(-d)])
            if name == "far":
                for d in APART:
                    arrive(("fy", 0, d), rows.at[16 + at_z(-d), :, half])
                    arrive(("fy", 1, d), rows.at[16 + at_z(-d), :, rest])
            whole = pl.ds(8 * r, NZ)
            acc[0:SLOTS, 0:256] = jnp.zeros((SLOTS, 256), F32)

            def one(cols):
                acc[0:SLOTS, 0:256] += trail(rows[whole, :, cols].reshape(SLOTS, TILE), wd[:, cols])

            tiled(one)
            grad = []
            for c in (0, 1):
                both = st[c, :, at_y(-r)].reshape(2 * SLOTS, 128)
                gate, up = dot(even, both), dot(odd, both)
                q = jax.nn.sigmoid(gate)
                hidden = acc[0:SLOTS, 128 * c : 128 * c + 128]
                grad.append(
                    (
                        (hidden * up * q * (1.0 + gate * (1.0 - q))).astype(BF),
                        (hidden * gate * q).astype(BF),
                    )
                )
            both = jnp.concatenate([grad[0][0], grad[1][0], grad[0][1], grad[1][1]], axis=1)

            def two(cols):
                part[whole, :, cols] = trail(both, wgu[cols, :]).astype(BF).reshape(NZ, PAIR, TILE)

            tiled(two)
            own[name] = local(part.at[8 * r + z], back.at[8 * r + z])
            for d in ORDER[1:]:
                send(("p", name, d), part.at[8 * r + at_z(-d)], back.at[8 * r + z], dev(-d, 0, 1))

        def combine(name):
            r = index[name]
            own[name].wait()
            for d in ORDER[1:]:
                arrive(("p", name, d), back.at[8 * r + at_z(d)])
            for c, table in enumerate(tables(r)):
                table = plain(table)
                if name == "near":
                    arrive(("e1", c), gets.at[2 + c])
                if name == "own":
                    arrive(("e2", c), gets.at[4 + c])

                def step(cols):
                    total = lead(table, back[pl.ds(8 * r, NZ), :, cols].reshape(SLOTS, TILE))
                    if name == "near":
                        total = total + gets[2 + c, :, cols].astype(F32)
                    if name == "own":
                        total = total + gets[4 + c, :, cols].astype(F32) + toks[0, c, :, cols].astype(F32)
                    sums[r, c, :, cols] = total.astype(BF)

                tiled(step)
                if name == "far":
                    send(("e1", c), sums.at[r, c], gets.at[2 + c], dev(0, side, 1))
                if name == "mid":
                    send(("e2", c), sums.at[r, c], gets.at[4 + c], dev(0, -side, 1))
                if name == "near":
                    send("end1", sums.at[r, c], gets.at[1], dev(0, side, c, pp_next), c)
                if name == "own":
                    send("end0", sums.at[r, c], gets.at[0], dev(0, 0, c, pp_next), c)

        order = ("far", "mid", "near", "own")
        for name in FLOW:
            compute(name)
        for name in order:
            combine(name)
        arrive("out", out_f.at[0])
        sent()

    arrive("end1", gets.at[1])
    arrive("end0", gets.at[0])

    def total(cols):
        out_b[0, :, cols] = (gets[0, :, cols].astype(F32) + gets[1, :, cols].astype(F32)).astype(BF)

    tiled(total)
    assert len(ids) <= N_SEM


def on_device(acts, grads, routes_f, routes_b, gates_f, gates_b, w_gate, w_up, w_down, stash):
    width = acts.shape[2]
    anywhere = pl.BlockSpec(memory_space=pl.ANY)
    inside = pl.BlockSpec(memory_space=pltpu.VMEM)
    out = jax.ShapeDtypeStruct((1, TOK, width), BF)
    chunks = pltpu.VMEM((NZ * NY, PAIR, width), BF)
    return pl.pallas_call(
        kernel,
        name="relay",
        out_shape=(out, out),
        in_specs=[anywhere] * 10,
        out_specs=(anywhere, inside),
        scratch_shapes=[
            chunks,
            chunks,
            chunks,
            chunks,
            pltpu.VMEM((NY, 2, TOK, width), BF),
            pltpu.VMEM((NY, 2, 2, TOK), jnp.int32),
            pltpu.VMEM((NY, 2, 2, TOK), F32),
            pltpu.VMEM((NY, 2, TOK, width), BF),
            pltpu.VMEM((6, TOK, width), BF),
            pltpu.VMEM((width, 512), BF),
            pltpu.VMEM((256, width), BF),
            pltpu.VMEM((2, NZ, NY, 32, 128), BF),
            pltpu.VMEM((256, 512), F32),
            pltpu.SemaphoreType.DMA((N_SEM,)),
            pltpu.SemaphoreType.DMA((N_SEM,)),
            pltpu.SemaphoreType.DMA((16,)),
            pltpu.SemaphoreType.REGULAR,
        ],
        compiler_params=pltpu.CompilerParams(
            collective_id=0, has_side_effects=True, vmem_limit_bytes=56 * 2**20
        ),
    )(
        acts, grads, routes_f[0].T, routes_b[0].T, gates_f[0].T, gates_b[0].T,
        w_gate, w_up, w_down, stash.reshape(NZ, NY, 32, 128),
    )


def solution(mesh):
    placed = (
        P("pp", "ep", None),
        P("pp", "ep", None),
        P("pp", "ep", None),
        P("pp", "ep", None),
        P("pp", "ep", None),
        P("pp", "ep", None),
        P("pp", None, "ep"),
        P("pp", None, "ep"),
        P("pp", "ep", None),
        P("pp", "ep", None, None, None, None),
    )
    return jax.shard_map(
        on_device,
        mesh=mesh,
        in_specs=placed,
        out_specs=(P("pp", "ep", None), P("pp", "ep", None)),
        check_vma=False,
    )
```

```python
import functools

import jax
import jax.numpy as jnp
from jax import lax
from jax.experimental import pallas as pl
from jax.experimental.pallas import tpu as pltpu
from jax.sharding import PartitionSpec as P

MESH = pl.DeviceIdType.MESH
BF = jnp.bfloat16
F32 = jnp.float32
TOK = 24
CAP = 8
PAIR = 16
NZ = 8
NY = 4
SLOTS = NZ * PAIR
TILE = 512
ORDER = (0, 1, 7, 2, 6, 3, 5, 4)
CLOSE = ORDER[1:7]
APART = ORDER[7:]
LAG = 2
GATE = 2
FLOW = ("mid", "near", "far", "own")
N_SEM = 208


def slot_table(routes, gates, shift, core):
    place = lax.broadcasted_iota(jnp.int32, (SLOTS, TOK), 0)
    expert = ((place >> 4) + shift) & 7
    mine = ((place >> 3) & 1) == core
    number = (place & 7).astype(F32)
    first = routes[0:1, :] == expert
    second = routes[1:2, :] == expert
    named = jnp.where(first | second, 1.0, 0.0).astype(BF)
    row = lax.broadcasted_iota(jnp.int32, (TOK, TOK), 0)
    col = lax.broadcasted_iota(jnp.int32, (TOK, TOK), 1)
    before = jnp.where(row < col, 1.0, 0.0).astype(BF)
    earlier = dot(named, before)
    here = (earlier == number) & mine
    return jnp.where(here & first, gates[0:1, :], 0.0) + jnp.where(here & second, gates[1:2, :], 0.0)


def split(table):
    high = table.astype(BF)
    return high, (table - high.astype(F32)).astype(BF)


def plain(table):
    return jnp.where(table > 0.0, 1.0, 0.0).astype(BF)


def lead(a, b):
    return lax.dot_general(a, b, (((0,), (0,)), ((), ())), preferred_element_type=F32)


def trail(a, b):
    return lax.dot_general(a, b, (((1,), (1,)), ((), ())), preferred_element_type=F32)


def dot(a, b):
    return jnp.dot(a, b, preferred_element_type=F32)


def kernel(
    acts, grads, routes_f, routes_b, gates_f, gates_b, w_gate, w_up, w_down, stash,
    out_f, ends,
    rows, part, back, slots, toks, named, scale, sums, gets, wgu, wd, st, acc,
    send_sem, recv_sem, local_sem, go,
):
    width = rows.shape[2]
    tiles = width // TILE
    pp, ep = lax.axis_index("pp"), lax.axis_index("ep")
    n_pp = lax.axis_size("pp")
    z, y, core = ep // 8, lax.rem(ep, 8) // 2, lax.rem(ep, 2)
    pp_next = lax.rem(pp + n_pp - 1, n_pp)
    pp_prev = lax.rem(pp + 1, n_pp)
    side = 2 * lax.rem(pp, 2) - 1
    mid, near = 2 - side, 2 + side

    def at_z(d):
        return lax.rem(z + d + NZ, NZ)

    def at_y(r):
        return lax.rem(y + r + NY, NY)

    def dev(d, r, c, section=None):
        return (pp if section is None else section, at_z(d) * 8 + at_y(r) * 2 + c)

    partner = dev(0, 0, 1 - core)

    ids, started, locals_ = {}, [], []

    def sem_of(key):
        return ids.setdefault(key, len(ids))

    def send(key, src, dst, target, lane=0):
        copy = pltpu.make_async_remote_copy(
            src_ref=src, dst_ref=dst, send_sem=send_sem.at[sem_of((key, lane) if lane else key)],
            recv_sem=recv_sem.at[sem_of(key)], device_id=target, device_id_type=MESH,
        )
        copy.start()
        started.append(copy)

    def arrive(key, dst):
        pltpu.make_async_remote_copy(
            src_ref=dst, dst_ref=dst, send_sem=send_sem.at[sem_of(key)],
            recv_sem=recv_sem.at[sem_of(key)], device_id=partner, device_id_type=MESH,
        ).wait_recv()

    def sent():
        for copy in started:
            copy.wait_send()
        started.clear()

    def local(src, dst):
        copy = pltpu.make_async_copy(src, dst, local_sem.at[len(locals_)])
        locals_.append(copy)
        copy.start()
        return copy

    def tiled(step):
        lax.fori_loop(0, tiles, lambda i, _: (step(pl.ds(pl.multiple_of(i * TILE, TILE), TILE)), 0)[1], 0)

    barrier = pltpu.get_barrier_semaphore()

    def greet(target):
        pl.semaphore_signal(barrier, inc=1, device_id=target, device_id_type=MESH)

    greet(partner)
    for d in range(1, NZ):
        greet(dev(d, 0, core))
    for r in (1, 3):
        greet(dev(0, r, core))
    greet(dev(0, 0, 1, pp_prev))
    greet(dev(0, side, 1, pp_prev))

    @pl.when(core == 0)
    def others():
        greet(dev(0, 0, 0, pp_prev))
        greet(dev(0, side, 0, pp_prev))

    @pl.when(core == 1)
    def across():
        greet(dev(0, 2, 1))

    def load_weights(c):
        cols = pl.ds(c * 128, 128)
        ups = pl.ds((2 + c) * 128, 128)
        return [
            local(w_gate.at[0], wgu.at[:, cols]),
            local(w_up.at[0], wgu.at[:, ups]),
            local(w_down.at[0], wd.at[pl.ds(c * 128, 128)]),
        ]

    def send_weights(c):
        send(("gate", c), w_gate.at[0], wgu.at[:, pl.ds(c * 128, 128)], partner)
        send(("up", c), w_up.at[0], wgu.at[:, pl.ds((2 + c) * 128, 128)], partner)
        send(("down", c), w_down.at[0], wd.at[pl.ds(c * 128, 128)], partner)

    def get_weights(c):
        arrive(("gate", c), wgu.at[:, pl.ds(c * 128, 128)])
        arrive(("up", c), wgu.at[:, pl.ds((2 + c) * 128, 128)])
        arrive(("down", c), wd.at[pl.ds(c * 128, 128)])

    def build(base, r, tables, weighted):
        left = []
        for c in (0, 1):
            left.append(split(tables[c]) if weighted else (plain(tables[c]),))

        def step(cols):
            total = None
            for c in (0, 1):
                for one in left[c]:
                    term = dot(one, toks[r, c, :, cols])
                    total = term if total is None else total + term
            slots[pl.ds(base, NZ), :, cols] = total.astype(BF).reshape(NZ, PAIR, TILE)

        tiled(step)

    @pl.when(core == 0)
    def forward():
        waits = [
            local(acts.at[0], toks.at[0, 0]),
            local(routes_f, named.at[0, 0]),
            local(gates_f, scale.at[0, 0]),
        ]
        mine = load_weights(0)
        pl.semaphore_wait(barrier, 12)
        send("routes_b", routes_b, named.at[0, 0], partner)
        send("gates_b", gates_b, scale.at[0, 0], partner)
        send("grads", grads.at[0], toks.at[0, 0], partner)
        send(("nextn", 0), routes_f, named.at[1, 0], dev(0, 0, 0, pp_next))
        send(("nexts", 0), gates_f, scale.at[1, 0], dev(0, 0, 0, pp_next))
        for copy in waits:
            copy.wait()
        arrive("routes_f", named.at[0, 1])
        arrive("gates_f", scale.at[0, 1])
        tables = [slot_table(named[0, c], scale[0, c], z, c) for c in (0, 1)]
        arrive("acts", toks.at[0, 1])

        build(0, 0, tables, False)

        def row(r, i):
            return (i // 4) * 16 + r * 4 + i % 4

        for i in range(1, NZ):
            d = ORDER[i]
            send(("zf", i), slots.at[d], rows.at[row(0, i)], dev(d, 0, 0))
        own = local(slots.at[0], rows.at[row(0, 0)])

        def spread(i):
            if i:
                arrive(("zf", i), rows.at[row(0, i)])
            if i == GATE:
                pl.semaphore_signal(go, inc=1, device_id=partner, device_id_type=MESH)
            source = rows.at[row(0, i)] if i else slots.at[0]
            send(("yp", i), source, rows.at[row(1, i)], dev(0, 1, 0))
            send(("ym", i), source, rows.at[row(3, i)], dev(0, 3, 0))

        def relay(i):
            arrive(("yp", i), rows.at[row(1, i)])
            arrive(("ym", i), rows.at[row(3, i)])
            if i % 2 == 0:
                send(("yy", i), rows.at[row(1, i)], rows.at[row(2, i)], dev(0, 1, 0))
            else:
                send(("yy", i), rows.at[row(3, i)], rows.at[row(2, i)], dev(0, 3, 0))

        def compute(h):
            for i in range(4 * h, 4 * h + 4):
                arrive(("yy", i), rows.at[row(2, i)])
            whole = pl.ds(16 * h, 16)
            acc[...] = jnp.zeros_like(acc)

            def one(cols):
                acc[...] += dot(rows[whole, :, cols].reshape(256, TILE), wgu[cols, :])

            tiled(one)
            gate, up = acc[:, :256], acc[:, 256:]
            hidden = (gate * jax.nn.sigmoid(gate) * up).astype(BF)

            def two(cols):
                part[whole, :, cols] = dot(hidden, wd[:, cols]).astype(BF).reshape(16, PAIR, TILE)

            tiled(two)

        def spot(g, r):
            return pl.ds(16 * (g // 2) + 2 * (g % 2) + 4 * r, 2)

        def land(g, n):
            return pl.ds(8 * g + 2 * n, 2)

        def reduce_first(g):
            send(("r2", g), part.at[spot(g, 2)], back.at[land(g, 0)], dev(0, side, 0))
            send(("rm", g), part.at[spot(g, mid)], back.at[land(g, 1)], dev(0, -side, 0))

        def reduce_second(g):
            for name, n, r, target in (("r2", 0, near, side), ("rm", 1, 0, 0)):
                arrive((name, g), back.at[land(g, n)])

                def add(cols):
                    total = part[spot(g, r), :, cols].astype(F32) + back[land(g, n), :, cols].astype(F32)
                    part[spot(g, r), :, cols] = total.astype(BF)

                tiled(add)
                send(("s" + name, g), part.at[spot(g, r)], back.at[land(g, 2 + n)], dev(0, target, 0, pp_next))

        def reduce_last(g):
            arrive(("sr2", g), back.at[land(g, 2)])
            arrive(("srm", g), back.at[land(g, 3)])
            for j in (1, 0):
                d = ORDER[2 * g + j]
                place = 16 if d == 0 else 8 + d

                def add(cols):
                    total = back[8 * g + 4 + j, :, cols].astype(F32) + back[8 * g + 6 + j, :, cols].astype(F32)
                    slots[place, :, cols] = total.astype(BF)

                tiled(add)
                if d:
                    send(("zr", d), slots.at[8 + d], slots.at[16 + d], dev(-d, 0, 0))

        for i in range(LAG):
            spread(i)
        send("stash", stash, st.at[0], partner)
        send_weights(0)
        for i in range(4):
            spread(i + LAG)
            relay(i)
        for i in range(4 + LAG, NZ):
            spread(i)
        send(("next", 0), acts.at[0], toks.at[1, 0], dev(0, 0, 0, pp_next))
        own.wait()
        for copy in mine:
            copy.wait()
        get_weights(1)
        compute(0)
        for i in range(4, 8):
            relay(i)
        reduce_first(0)
        reduce_first(1)
        compute(1)
        reduce_second(0)
        reduce_second(1)
        reduce_first(2)
        reduce_first(3)
        reduce_last(0)
        reduce_second(2)
        reduce_last(1)
        reduce_second(3)
        reduce_last(2)
        reduce_last(3)
        for c in (0, 1):
            arrive(("next", c), toks.at[1, c])
            arrive(("nextn", c), named.at[1, c])
            arrive(("nexts", c), scale.at[1, c])
        left = [split(slot_table(named[1, c], scale[1, c], z, c)) for c in (0, 1)]
        for d in range(1, NZ):
            arrive(("zr", d), slots.at[16 + d])
        for c in (1, 0):
            high, low = left[c]

            def step(cols):
                got = slots[pl.ds(16, NZ), :, cols].reshape(SLOTS, TILE)
                total = toks[1, c, :, cols].astype(F32) + lead(high, got) + lead(low, got)
                sums[0, c, :, cols] = total.astype(BF)

            tiled(step)
            if c:
                send("out", sums.at[0, 1], out_f.at[0], partner)
            else:
                last = local(sums.at[0, 0], out_f.at[0])
        last.wait()
        sent()

    locals_.clear()

    @pl.when(core == 1)
    def backward():
        waits = [
            local(grads.at[0], toks.at[0, 1]),
            local(routes_b, named.at[0, 1]),
            local(gates_b, scale.at[0, 1]),
        ]
        keep = local(stash, st.at[1])
        mine = load_weights(1)
        pl.semaphore_wait(barrier, 15)
        send("routes_f", routes_f, named.at[0, 1], partner)
        send("gates_f", gates_f, scale.at[0, 1], partner)
        send("acts", acts.at[0], toks.at[0, 1], partner)
        send(("tm", 1), grads.at[0], toks.at[mid, 1], dev(0, side, 1))
        send(("tn", 1), grads.at[0], toks.at[near, 1], dev(0, -side, 1))
        for copy in waits:
            copy.wait()
        arrive("routes_b", named.at[0, 0])
        arrive("gates_b", scale.at[0, 0])
        for name, r, target in (("mid", mid, side), ("near", near, -side), ("far", 2, 2)):
            send(("nr", name), named.at[0], named.at[r], dev(0, target, 1))
            send(("ng", name), scale.at[0], scale.at[r], dev(0, target, 1))
        arrive("grads", toks.at[0, 0])
        send(("tm", 0), toks.at[0, 0], toks.at[mid, 0], dev(0, side, 1))
        send(("tn", 0), toks.at[0, 0], toks.at[near, 0], dev(0, -side, 1))
        own = {}
        index = {"own": 0, "mid": mid, "near": near, "far": 2}

        def tables(r):
            return [slot_table(named[r, c], scale[r, c], 0, c) for c in (0, 1)]

        def scatter(name):
            r = index[name]
            if name != "own":
                arrive(("nr", name), named.at[r])
                arrive(("ng", name), scale.at[r])
            build(8 * r, r, tables(r), True)
            own[name] = local(slots.at[8 * r + z], rows.at[8 * r + z])
            if name == "own" and GATE >= 0:
                pl.semaphore_wait(go, 1)
            for d in (APART + CLOSE if name == "own" else CLOSE):
                send(("c", name, d), slots.at[8 * r + at_z(d)], rows.at[8 * r + z], dev(d, 0, 1))

        scatter("own")
        send_weights(1)
        arrive(("tm", 0), toks.at[mid, 0])
        arrive(("tm", 1), toks.at[mid, 1])
        send(("ty", 0), toks.at[mid, 0], toks.at[2, 0], dev(0, side, 1))
        arrive(("tn", 0), toks.at[near, 0])
        arrive(("tn", 1), toks.at[near, 1])
        send(("ty", 1), toks.at[near, 1], toks.at[2, 1], dev(0, -side, 1))
        send(("next", 1), acts.at[0], toks.at[1, 1], dev(0, 0, 0, pp_next))
        send(("nextn", 1), routes_f, named.at[1, 1], dev(0, 0, 0, pp_next))
        send(("nexts", 1), gates_f, scale.at[1, 1], dev(0, 0, 0, pp_next))
        scatter("mid")
        scatter("near")
        arrive(("ty", 0), toks.at[2, 0])
        arrive(("ty", 1), toks.at[2, 1])
        scatter("far")

        half = pl.ds(0, width // 2)
        rest = pl.ds(width // 2, width // 2)
        for d in APART:
            source = at_z(-d)
            arrive(("c", "own", d), rows.at[source])
            send(("fp", d), rows.at[source], rows.at[8 * mid + source], dev(0, side, 1))
            send(("fm", d), rows.at[source], rows.at[8 * near + source], dev(0, -side, 1))
        for d in APART:
            source = at_z(-d)
            arrive(("fp", d), rows.at[8 * mid + source])
            send(("fy", 0, d), rows.at[8 * mid + source, :, half], rows.at[16 + source, :, half], dev(0, side, 1))
            arrive(("fm", d), rows.at[8 * near + source])
            send(("fy", 1, d), rows.at[8 * near + source, :, rest], rows.at[16 + source, :, rest], dev(0, -side, 1))

        for copy in mine:
            copy.wait()
        keep.wait()
        get_weights(0)
        arrive("stash", st.at[0])
        pick_row = lax.broadcasted_iota(jnp.int32, (SLOTS, 2 * SLOTS), 0)
        pick_col = lax.broadcasted_iota(jnp.int32, (SLOTS, 2 * SLOTS), 1)
        even = jnp.where(pick_col == 2 * pick_row, 1.0, 0.0).astype(BF)
        odd = jnp.where(pick_col == 2 * pick_row + 1, 1.0, 0.0).astype(BF)

        def compute(name):
            r = index[name]
            own[name].wait()
            for d in CLOSE:
                arrive(("c", name, d), rows.at[8 * r + at_z(-d)])
            if name == "far":
                for d in APART:
                    arrive(("fy", 0, d), rows.at[16 + at_z(-d), :, half])
                    arrive(("fy", 1, d), rows.at[16 + at_z(-d), :, rest])
            whole = pl.ds(8 * r, NZ)
            acc[0:SLOTS, 0:256] = jnp.zeros((SLOTS, 256), F32)

            def one(cols):
                acc[0:SLOTS, 0:256] += trail(rows[whole, :, cols].reshape(SLOTS, TILE), wd[:, cols])

            tiled(one)
            grad = []
            for c in (0, 1):
                both = st[c, :, at_y(-r)].reshape(2 * SLOTS, 128)
                gate, up = dot(even, both), dot(odd, both)
                q = jax.nn.sigmoid(gate)
                hidden = acc[0:SLOTS, 128 * c : 128 * c + 128]
                grad.append(
                    (
                        (hidden * up * q * (1.0 + gate * (1.0 - q))).astype(BF),
                        (hidden * gate * q).astype(BF),
                    )
                )
            both = jnp.concatenate([grad[0][0], grad[1][0], grad[0][1], grad[1][1]], axis=1)

            def two(cols):
                part[whole, :, cols] = trail(both, wgu[cols, :]).astype(BF).reshape(NZ, PAIR, TILE)

            tiled(two)
            own[name] = local(part.at[8 * r + z], back.at[8 * r + z])
            for d in ORDER[:0:-1]:
                send(("p", name, d), part.at[8 * r + at_z(-d)], back.at[8 * r + z], dev(-d, 0, 1))

        def combine(name):
            r = index[name]
            own[name].wait()
            for d in ORDER[1:]:
                arrive(("p", name, d), back.at[8 * r + at_z(d)])
            for c, table in enumerate(tables(r)):
                table = plain(table)
                if name == "near":
                    arrive(("e1", c), gets.at[c])
                if name == "own":
                    arrive(("e2", c), gets.at[2 + c])

                def step(cols):
                    total = lead(table, back[pl.ds(8 * r, NZ), :, cols].reshape(SLOTS, TILE))
                    if name == "near":
                        total = total + gets[c, :, cols].astype(F32)
                    if name == "own":
                        total = total + gets[2 + c, :, cols].astype(F32) + toks[0, c, :, cols].astype(F32)
                    sums[r, c, :, cols] = total.astype(BF)

                tiled(step)
                if name == "far":
                    send(("e1", c), sums.at[r, c], gets.at[c], dev(0, side, 1))
                if name == "mid":
                    send(("e2", c), sums.at[r, c], gets.at[2 + c], dev(0, -side, 1))
                if name == "near":
                    send("end1", sums.at[r, c], ends.at[1], dev(0, side, c, pp_next), c)
                if name == "own":
                    send("end0", sums.at[r, c], ends.at[0], dev(0, 0, c, pp_next), c)

        order = ("far", "mid", "near", "own")
        for name in FLOW:
            compute(name)
        for name in order:
            combine(name)
        arrive("out", out_f.at[0])
        sent()

    arrive("end1", ends.at[1])
    arrive("end0", ends.at[0])
    assert len(ids) <= N_SEM


def on_device(acts, grads, routes_f, routes_b, gates_f, gates_b, w_gate, w_up, w_down, stash):
    width = acts.shape[2]
    anywhere = pl.BlockSpec(memory_space=pl.ANY)
    out = jax.ShapeDtypeStruct((1, TOK, width), BF)
    chunks = pltpu.VMEM((NZ * NY, PAIR, width), BF)
    out, ends = pl.pallas_call(
        kernel,
        name="relay",
        out_shape=(out, jax.ShapeDtypeStruct((2, TOK, width), BF)),
        in_specs=[anywhere] * 10,
        out_specs=(anywhere, anywhere),
        scratch_shapes=[
            chunks,
            chunks,
            chunks,
            chunks,
            pltpu.VMEM((NY, 2, TOK, width), BF),
            pltpu.VMEM((NY, 2, 2, TOK), jnp.int32),
            pltpu.VMEM((NY, 2, 2, TOK), F32),
            pltpu.VMEM((NY, 2, TOK, width), BF),
            pltpu.VMEM((4, TOK, width), BF),
            pltpu.VMEM((width, 512), BF),
            pltpu.VMEM((256, width), BF),
            pltpu.VMEM((2, NZ, NY, 32, 128), BF),
            pltpu.VMEM((256, 512), F32),
            pltpu.SemaphoreType.DMA((N_SEM,)),
            pltpu.SemaphoreType.DMA((N_SEM,)),
            pltpu.SemaphoreType.DMA((16,)),
            pltpu.SemaphoreType.REGULAR,
        ],
        compiler_params=pltpu.CompilerParams(
            collective_id=0, has_side_effects=True, vmem_limit_bytes=56 * 2**20
        ),
    )(
        acts, grads, routes_f[0].T, routes_b[0].T, gates_f[0].T, gates_b[0].T,
        w_gate, w_up, w_down, stash.reshape(NZ, NY, 32, 128),
    )
    return out, (ends[0:1].astype(F32) + ends[1:2].astype(F32)).astype(BF)


def solution(mesh):
    placed = (
        P("pp", "ep", None),
        P("pp", "ep", None),
        P("pp", "ep", None),
        P("pp", "ep", None),
        P("pp", "ep", None),
        P("pp", "ep", None),
        P("pp", None, "ep"),
        P("pp", None, "ep"),
        P("pp", "ep", None),
        P("pp", "ep", None, None, None, None),
    )
    return jax.shard_map(
        on_device,
        mesh=mesh,
        in_specs=placed,
        out_specs=(P("pp", "ep", None), P("pp", "ep", None)),
        check_vma=False,
    )
```

```python
import functools

import jax
import jax.numpy as jnp
from jax import lax
from jax.experimental import pallas as pl
from jax.experimental.pallas import tpu as pltpu
from jax.sharding import PartitionSpec as P

MESH = pl.DeviceIdType.MESH
BF = jnp.bfloat16
F32 = jnp.float32
TOK = 24
CAP = 8
PAIR = 16
NZ = 8
NY = 4
SLOTS = NZ * PAIR
TILE = 512
ORDER = (0, 1, 7, 2, 6, 3, 5, 4)
CLOSE = ORDER[1:7]
APART = ORDER[7:]
LAG = 2
GATE = 2
FLOW = ("mid", "near", "far", "own")
N_SEM = 208


def slot_table(routes, gates, shift, core):
    place = lax.broadcasted_iota(jnp.int32, (SLOTS, TOK), 0)
    expert = ((place >> 4) + shift) & 7
    mine = ((place >> 3) & 1) == core
    number = (place & 7).astype(F32)
    first = routes[0:1, :] == expert
    second = routes[1:2, :] == expert
    named = jnp.where(first | second, 1.0, 0.0).astype(BF)
    row = lax.broadcasted_iota(jnp.int32, (TOK, TOK), 0)
    col = lax.broadcasted_iota(jnp.int32, (TOK, TOK), 1)
    before = jnp.where(row < col, 1.0, 0.0).astype(BF)
    earlier = dot(named, before)
    here = (earlier == number) & mine
    return jnp.where(here & first, gates[0:1, :], 0.0) + jnp.where(here & second, gates[1:2, :], 0.0)


def split(table):
    high = table.astype(BF)
    return high, (table - high.astype(F32)).astype(BF)


def plain(table):
    return jnp.where(table > 0.0, 1.0, 0.0).astype(BF)


def lead(a, b):
    return lax.dot_general(a, b, (((0,), (0,)), ((), ())), preferred_element_type=F32)


def trail(a, b):
    return lax.dot_general(a, b, (((1,), (1,)), ((), ())), preferred_element_type=F32)


def dot(a, b):
    return jnp.dot(a, b, preferred_element_type=F32)


def kernel(
    acts, grads, routes_f, routes_b, gates_f, gates_b, w_gate, w_up, w_down, stash,
    out_f, ends,
    rows, part, back, slots, toks, named, scale, sums, gets, wgu, wd, st, acc,
    send_sem, recv_sem, local_sem, go,
):
    width = rows.shape[2]
    tiles = width // TILE
    cuts = ((0, tiles // 2), (tiles // 2, tiles))
    pp, ep = lax.axis_index("pp"), lax.axis_index("ep")
    n_pp = lax.axis_size("pp")
    z, y, core = ep // 8, lax.rem(ep, 8) // 2, lax.rem(ep, 2)
    pp_next = lax.rem(pp + n_pp - 1, n_pp)
    pp_prev = lax.rem(pp + 1, n_pp)
    side = 2 * lax.rem(pp, 2) - 1
    mid, near = 2 - side, 2 + side

    def at_z(d):
        return lax.rem(z + d + NZ, NZ)

    def at_y(r):
        return lax.rem(y + r + NY, NY)

    def dev(d, r, c, section=None):
        return (pp if section is None else section, at_z(d) * 8 + at_y(r) * 2 + c)

    partner = dev(0, 0, 1 - core)

    ids, started, locals_ = {}, [], []

    def sem_of(key):
        return ids.setdefault(key, len(ids))

    def send(key, src, dst, target, lane=0):
        copy = pltpu.make_async_remote_copy(
            src_ref=src, dst_ref=dst, send_sem=send_sem.at[sem_of((key, lane) if lane else key)],
            recv_sem=recv_sem.at[sem_of(key)], device_id=target, device_id_type=MESH,
        )
        copy.start()
        started.append(copy)

    def arrive(key, dst):
        pltpu.make_async_remote_copy(
            src_ref=dst, dst_ref=dst, send_sem=send_sem.at[sem_of(key)],
            recv_sem=recv_sem.at[sem_of(key)], device_id=partner, device_id_type=MESH,
        ).wait_recv()

    def sent():
        for copy in started:
            copy.wait_send()
        started.clear()

    def local(src, dst):
        copy = pltpu.make_async_copy(src, dst, local_sem.at[len(locals_)])
        locals_.append(copy)
        copy.start()
        return copy

    def tiled(step, first=0, last=tiles):
        lax.fori_loop(first, last, lambda i, _: (step(pl.ds(pl.multiple_of(i * TILE, TILE), TILE)), 0)[1], 0)

    barrier = pltpu.get_barrier_semaphore()

    def greet(target):
        pl.semaphore_signal(barrier, inc=1, device_id=target, device_id_type=MESH)

    greet(partner)
    for d in range(1, NZ):
        greet(dev(d, 0, core))
    for r in (1, 3):
        greet(dev(0, r, core))
    greet(dev(0, 0, 1, pp_prev))
    greet(dev(0, side, 1, pp_prev))

    @pl.when(core == 0)
    def others():
        greet(dev(0, 0, 0, pp_prev))
        greet(dev(0, side, 0, pp_prev))

    @pl.when(core == 1)
    def across():
        greet(dev(0, 2, 1))

    def load_weights(c):
        cols = pl.ds(c * 128, 128)
        ups = pl.ds((2 + c) * 128, 128)
        return [
            local(w_gate.at[0], wgu.at[:, cols]),
            local(w_up.at[0], wgu.at[:, ups]),
            local(w_down.at[0], wd.at[pl.ds(c * 128, 128)]),
        ]

    def send_weights(c):
        send(("gate", c), w_gate.at[0], wgu.at[:, pl.ds(c * 128, 128)], partner)
        send(("up", c), w_up.at[0], wgu.at[:, pl.ds((2 + c) * 128, 128)], partner)
        send(("down", c), w_down.at[0], wd.at[pl.ds(c * 128, 128)], partner)

    def get_weights(c):
        arrive(("gate", c), wgu.at[:, pl.ds(c * 128, 128)])
        arrive(("up", c), wgu.at[:, pl.ds((2 + c) * 128, 128)])
        arrive(("down", c), wd.at[pl.ds(c * 128, 128)])

    def build(base, r, tables, weighted):
        left = []
        for c in (0, 1):
            left.append(split(tables[c]) if weighted else (plain(tables[c]),))

        def step(cols):
            total = None
            for c in (0, 1):
                for one in left[c]:
                    term = dot(one, toks[r, c, :, cols])
                    total = term if total is None else total + term
            slots[pl.ds(base, NZ), :, cols] = total.astype(BF).reshape(NZ, PAIR, TILE)

        tiled(step)

    @pl.when(core == 0)
    def forward():
        waits = [
            local(acts.at[0], toks.at[0, 0]),
            local(routes_f, named.at[0, 0]),
            local(gates_f, scale.at[0, 0]),
        ]
        mine = load_weights(0)
        pl.semaphore_wait(barrier, 12)
        send("routes_b", routes_b, named.at[0, 0], partner)
        send("gates_b", gates_b, scale.at[0, 0], partner)
        send("grads", grads.at[0], toks.at[0, 0], partner)
        send(("nextn", 0), routes_f, named.at[1, 0], dev(0, 0, 0, pp_next))
        send(("nexts", 0), gates_f, scale.at[1, 0], dev(0, 0, 0, pp_next))
        for copy in waits:
            copy.wait()
        arrive("routes_f", named.at[0, 1])
        arrive("gates_f", scale.at[0, 1])
        tables = [slot_table(named[0, c], scale[0, c], z, c) for c in (0, 1)]
        arrive("acts", toks.at[0, 1])

        build(0, 0, tables, False)

        def row(r, i):
            return (i // 4) * 16 + r * 4 + i % 4

        for i in range(1, NZ):
            d = ORDER[i]
            send(("zf", i), slots.at[d], rows.at[row(0, i)], dev(d, 0, 0))
        own = local(slots.at[0], rows.at[row(0, 0)])

        def spread(i):
            if i:
                arrive(("zf", i), rows.at[row(0, i)])
            if i == GATE:
                pl.semaphore_signal(go, inc=1, device_id=partner, device_id_type=MESH)
            source = rows.at[row(0, i)] if i else slots.at[0]
            send(("yp", i), source, rows.at[row(1, i)], dev(0, 1, 0))
            send(("ym", i), source, rows.at[row(3, i)], dev(0, 3, 0))

        def relay(i):
            arrive(("yp", i), rows.at[row(1, i)])
            arrive(("ym", i), rows.at[row(3, i)])
            if i % 2 == 0:
                send(("yy", i), rows.at[row(1, i)], rows.at[row(2, i)], dev(0, 1, 0))
            else:
                send(("yy", i), rows.at[row(3, i)], rows.at[row(2, i)], dev(0, 3, 0))

        def compute(h):
            for i in range(4 * h, 4 * h + 4):
                arrive(("yy", i), rows.at[row(2, i)])
            whole = pl.ds(16 * h, 16)
            acc[...] = jnp.zeros_like(acc)

            def one(cols):
                acc[...] += dot(rows[whole, :, cols].reshape(256, TILE), wgu[cols, :])

            tiled(one)
            gate, up = acc[:, :256], acc[:, 256:]
            hidden = (gate * jax.nn.sigmoid(gate) * up).astype(BF)

            def two(cols):
                part[whole, :, cols] = dot(hidden, wd[:, cols]).astype(BF).reshape(16, PAIR, TILE)

            tiled(two)

        def spot(g, r):
            return pl.ds(16 * (g // 2) + 2 * (g % 2) + 4 * r, 2)

        def land(g, n):
            return pl.ds(8 * g + 2 * n, 2)

        def reduce_first(g):
            send(("r2", g), part.at[spot(g, 2)], back.at[land(g, 0)], dev(0, side, 0))
            send(("rm", g), part.at[spot(g, mid)], back.at[land(g, 1)], dev(0, -side, 0))

        def reduce_second(g):
            for name, n, r, target in (("r2", 0, near, side), ("rm", 1, 0, 0)):
                arrive((name, g), back.at[land(g, n)])

                def add(cols):
                    total = part[spot(g, r), :, cols].astype(F32) + back[land(g, n), :, cols].astype(F32)
                    part[spot(g, r), :, cols] = total.astype(BF)

                tiled(add)
                send(("s" + name, g), part.at[spot(g, r)], back.at[land(g, 2 + n)], dev(0, target, 0, pp_next))

        def reduce_last(g):
            arrive(("sr2", g), back.at[land(g, 2)])
            arrive(("srm", g), back.at[land(g, 3)])
            for j in (1, 0):
                d = ORDER[2 * g + j]
                place = 16 if d == 0 else 8 + d

                def add(cols):
                    total = back[8 * g + 4 + j, :, cols].astype(F32) + back[8 * g + 6 + j, :, cols].astype(F32)
                    slots[place, :, cols] = total.astype(BF)

                tiled(add)
                if d:
                    send(("zr", d), slots.at[8 + d], slots.at[16 + d], dev(-d, 0, 0))

        for i in range(LAG):
            spread(i)
        send("stash", stash, st.at[0], partner)
        send_weights(0)
        for i in range(4):
            spread(i + LAG)
            relay(i)
        for i in range(4 + LAG, NZ):
            spread(i)
        send(("next", 0), acts.at[0], toks.at[1, 0], dev(0, 0, 0, pp_next))
        own.wait()
        for copy in mine:
            copy.wait()
        get_weights(1)
        compute(0)
        for i in range(4, 8):
            relay(i)
        reduce_first(0)
        reduce_first(1)
        compute(1)
        reduce_second(0)
        reduce_second(1)
        reduce_first(2)
        reduce_first(3)
        reduce_last(0)
        reduce_second(2)
        reduce_last(1)
        reduce_second(3)
        reduce_last(2)
        reduce_last(3)
        for c in (0, 1):
            arrive(("next", c), toks.at[1, c])
            arrive(("nextn", c), named.at[1, c])
            arrive(("nexts", c), scale.at[1, c])
        left = [split(slot_table(named[1, c], scale[1, c], z, c)) for c in (0, 1)]
        for d in range(1, NZ):
            arrive(("zr", d), slots.at[16 + d])
        for c in (1, 0):
            high, low = left[c]

            def step(cols):
                got = slots[pl.ds(16, NZ), :, cols].reshape(SLOTS, TILE)
                total = toks[1, c, :, cols].astype(F32) + lead(high, got) + lead(low, got)
                sums[0, c, :, cols] = total.astype(BF)

            tiled(step)
            if c:
                send("out", sums.at[0, 1], out_f.at[0], partner)
            else:
                last = local(sums.at[0, 0], out_f.at[0])
        last.wait()
        sent()

    locals_.clear()

    @pl.when(core == 1)
    def backward():
        waits = [
            local(grads.at[0], toks.at[0, 1]),
            local(routes_b, named.at[0, 1]),
            local(gates_b, scale.at[0, 1]),
        ]
        keep = local(stash, st.at[1])
        mine = load_weights(1)
        pl.semaphore_wait(barrier, 15)
        send("routes_f", routes_f, named.at[0, 1], partner)
        send("gates_f", gates_f, scale.at[0, 1], partner)
        send("acts", acts.at[0], toks.at[0, 1], partner)
        send(("tm", 1), grads.at[0], toks.at[mid, 1], dev(0, side, 1))
        send(("tn", 1), grads.at[0], toks.at[near, 1], dev(0, -side, 1))
        for copy in waits:
            copy.wait()
        arrive("routes_b", named.at[0, 0])
        arrive("gates_b", scale.at[0, 0])
        for name, r, target in (("mid", mid, side), ("near", near, -side), ("far", 2, 2)):
            send(("nr", name), named.at[0], named.at[r], dev(0, target, 1))
            send(("ng", name), scale.at[0], scale.at[r], dev(0, target, 1))
        arrive("grads", toks.at[0, 0])
        send(("tm", 0), toks.at[0, 0], toks.at[mid, 0], dev(0, side, 1))
        send(("tn", 0), toks.at[0, 0], toks.at[near, 0], dev(0, -side, 1))
        own = {}
        index = {"own": 0, "mid": mid, "near": near, "far": 2}

        def tables(r):
            return [slot_table(named[r, c], scale[r, c], 0, c) for c in (0, 1)]

        def scatter(name):
            r = index[name]
            if name != "own":
                arrive(("nr", name), named.at[r])
                arrive(("ng", name), scale.at[r])
            build(8 * r, r, tables(r), True)
            own[name] = local(slots.at[8 * r + z], rows.at[8 * r + z])
            if name == "own" and GATE >= 0:
                pl.semaphore_wait(go, 1)
            for d in (APART + CLOSE if name == "own" else CLOSE):
                send(("c", name, d), slots.at[8 * r + at_z(d)], rows.at[8 * r + z], dev(d, 0, 1))

        scatter("own")
        send_weights(1)
        arrive(("tm", 0), toks.at[mid, 0])
        arrive(("tm", 1), toks.at[mid, 1])
        send(("ty", 0), toks.at[mid, 0], toks.at[2, 0], dev(0, side, 1))
        arrive(("tn", 0), toks.at[near, 0])
        arrive(("tn", 1), toks.at[near, 1])
        send(("ty", 1), toks.at[near, 1], toks.at[2, 1], dev(0, -side, 1))
        send(("next", 1), acts.at[0], toks.at[1, 1], dev(0, 0, 0, pp_next))
        send(("nextn", 1), routes_f, named.at[1, 1], dev(0, 0, 0, pp_next))
        send(("nexts", 1), gates_f, scale.at[1, 1], dev(0, 0, 0, pp_next))
        scatter("mid")
        scatter("near")
        arrive(("ty", 0), toks.at[2, 0])
        arrive(("ty", 1), toks.at[2, 1])
        scatter("far")

        half = pl.ds(0, width // 2)
        rest = pl.ds(width // 2, width // 2)
        for d in APART:
            source = at_z(-d)
            arrive(("c", "own", d), rows.at[source])
            send(("fp", d), rows.at[source], rows.at[8 * mid + source], dev(0, side, 1))
            send(("fm", d), rows.at[source], rows.at[8 * near + source], dev(0, -side, 1))
        for d in APART:
            source = at_z(-d)
            arrive(("fp", d), rows.at[8 * mid + source])
            send(("fy", 0, d), rows.at[8 * mid + source, :, half], rows.at[16 + source, :, half], dev(0, side, 1))
            arrive(("fm", d), rows.at[8 * near + source])
            send(("fy", 1, d), rows.at[8 * near + source, :, rest], rows.at[16 + source, :, rest], dev(0, -side, 1))

        for copy in mine:
            copy.wait()
        keep.wait()
        get_weights(0)
        arrive("stash", st.at[0])
        pick_row = lax.broadcasted_iota(jnp.int32, (SLOTS, 2 * SLOTS), 0)
        pick_col = lax.broadcasted_iota(jnp.int32, (SLOTS, 2 * SLOTS), 1)
        even = jnp.where(pick_col == 2 * pick_row, 1.0, 0.0).astype(BF)
        odd = jnp.where(pick_col == 2 * pick_row + 1, 1.0, 0.0).astype(BF)

        def compute(name):
            r = index[name]
            own[name].wait()
            for d in CLOSE:
                arrive(("c", name, d), rows.at[8 * r + at_z(-d)])
            if name == "far":
                for d in APART:
                    arrive(("fy", 0, d), rows.at[16 + at_z(-d), :, half])
                    arrive(("fy", 1, d), rows.at[16 + at_z(-d), :, rest])
            whole = pl.ds(8 * r, NZ)
            acc[0:SLOTS, 0:256] = jnp.zeros((SLOTS, 256), F32)

            def one(cols):
                acc[0:SLOTS, 0:256] += trail(rows[whole, :, cols].reshape(SLOTS, TILE), wd[:, cols])

            tiled(one)
            grad = []
            for c in (0, 1):
                both = st[c, :, at_y(-r)].reshape(2 * SLOTS, 128)
                gate, up = dot(even, both), dot(odd, both)
                q = jax.nn.sigmoid(gate)
                hidden = acc[0:SLOTS, 128 * c : 128 * c + 128]
                grad.append(
                    (
                        (hidden * up * q * (1.0 + gate * (1.0 - q))).astype(BF),
                        (hidden * gate * q).astype(BF),
                    )
                )
            both = jnp.concatenate([grad[0][0], grad[1][0], grad[0][1], grad[1][1]], axis=1)

            def two(cols):
                part[whole, :, cols] = trail(both, wgu[cols, :]).astype(BF).reshape(NZ, PAIR, TILE)

            tiled(two)
            own[name] = local(part.at[8 * r + z], back.at[8 * r + z])
            for d in ORDER[:0:-1]:
                send(("p", name, d), part.at[8 * r + at_z(-d)], back.at[8 * r + z], dev(-d, 0, 1))

        def combine(name):
            r = index[name]
            own[name].wait()
            for d in ORDER[1:]:
                arrive(("p", name, d), back.at[8 * r + at_z(d)])
            for c, table in enumerate(tables(r)):
                table = plain(table)
                if name == "near":
                    arrive(("e1", c), gets.at[c])
                if name == "own":
                    arrive(("e2", c), gets.at[2 + c])

                def step(cols):
                    total = lead(table, back[pl.ds(8 * r, NZ), :, cols].reshape(SLOTS, TILE))
                    if name == "near":
                        total = total + gets[c, :, cols].astype(F32)
                    if name == "own":
                        total = total + gets[2 + c, :, cols].astype(F32) + toks[0, c, :, cols].astype(F32)
                    sums[r, c, :, cols] = total.astype(BF)

                if name == "own":
                    for n, (first, last) in enumerate(cuts):
                        tiled(step, first, last)
                        cols = pl.ds(first * TILE, (last - first) * TILE)
                        send(
                            ("end0", n), sums.at[r, c, :, cols], ends.at[0, :, cols],
                            dev(0, 0, c, pp_next), c,
                        )
                    continue
                tiled(step)
                if name == "far":
                    send(("e1", c), sums.at[r, c], gets.at[c], dev(0, side, 1))
                if name == "mid":
                    send(("e2", c), sums.at[r, c], gets.at[2 + c], dev(0, -side, 1))
                if name == "near":
                    send("end1", sums.at[r, c], ends.at[1], dev(0, side, c, pp_next), c)

        order = ("far", "mid", "near", "own")
        for name in FLOW:
            compute(name)
        for name in order:
            combine(name)
        arrive("out", out_f.at[0])
        sent()

    arrive("end1", ends.at[1])
    for n, (first, last) in enumerate(cuts):
        arrive(("end0", n), ends.at[0, :, pl.ds(first * TILE, (last - first) * TILE)])
    assert len(ids) <= N_SEM


def on_device(acts, grads, routes_f, routes_b, gates_f, gates_b, w_gate, w_up, w_down, stash):
    width = acts.shape[2]
    anywhere = pl.BlockSpec(memory_space=pl.ANY)
    out = jax.ShapeDtypeStruct((1, TOK, width), BF)
    chunks = pltpu.VMEM((NZ * NY, PAIR, width), BF)
    out, ends = pl.pallas_call(
        kernel,
        name="relay",
        out_shape=(out, jax.ShapeDtypeStruct((2, TOK, width), BF)),
        in_specs=[anywhere] * 10,
        out_specs=(anywhere, anywhere),
        scratch_shapes=[
            chunks,
            chunks,
            chunks,
            chunks,
            pltpu.VMEM((NY, 2, TOK, width), BF),
            pltpu.VMEM((NY, 2, 2, TOK), jnp.int32),
            pltpu.VMEM((NY, 2, 2, TOK), F32),
            pltpu.VMEM((NY, 2, TOK, width), BF),
            pltpu.VMEM((4, TOK, width), BF),
            pltpu.VMEM((width, 512), BF),
            pltpu.VMEM((256, width), BF),
            pltpu.VMEM((2, NZ, NY, 32, 128), BF),
            pltpu.VMEM((256, 512), F32),
            pltpu.SemaphoreType.DMA((N_SEM,)),
            pltpu.SemaphoreType.DMA((N_SEM,)),
            pltpu.SemaphoreType.DMA((16,)),
            pltpu.SemaphoreType.REGULAR,
        ],
        compiler_params=pltpu.CompilerParams(
            collective_id=0, has_side_effects=True, vmem_limit_bytes=56 * 2**20
        ),
    )(
        acts, grads, routes_f[0].T, routes_b[0].T, gates_f[0].T, gates_b[0].T,
        w_gate, w_up, w_down, stash.reshape(NZ, NY, 32, 128),
    )
    return out, (ends[0:1].astype(F32) + ends[1:2].astype(F32)).astype(BF)


def solution(mesh):
    placed = (
        P("pp", "ep", None),
        P("pp", "ep", None),
        P("pp", "ep", None),
        P("pp", "ep", None),
        P("pp", "ep", None),
        P("pp", "ep", None),
        P("pp", None, "ep"),
        P("pp", None, "ep"),
        P("pp", "ep", None),
        P("pp", "ep", None, None, None, None),
    )
    return jax.shard_map(
        on_device,
        mesh=mesh,
        in_specs=placed,
        out_specs=(P("pp", "ep", None), P("pp", "ep", None)),
        check_vma=False,
    )
```
